256 devices in a mesh: dp: 16 (over y, x_hi, core), ctx: 16 (over x_lo, z).
Axes of the slice: x: 4 (x_hi: 2, x_lo: 2; x = x_hi * 2 + x_lo), y: 4, z: 8, core: 2. Of those that a mesh axis runs over, the one named last changes fastest.
Arguments:
- queries: bfloat16 [16, 2048, 3584], P('dp', 'ctx'), may hold values from -8 to 8
- keys: bfloat16 [16, 2048, 512], P('dp', 'ctx'), may hold values from -8 to 8
- values: bfloat16 [16, 2048, 512], P('dp', 'ctx'), may hold values from -6 to 6
- out_grad: bfloat16 [16, 2048, 3584], P('dp', 'ctx'), may hold values from -6 to 6
- routes: int32 [16, 2048], P('dp', 'ctx'), may hold values from -1 to 16383, as said below
- per_head_scale: float32 [28], replicated, may hold values from 0.5 to 2
Outputs:
- query_grad: bfloat16 [16, 2048, 3584], P('dp', 'ctx')
- key_grad: bfloat16 [16, 2048, 512], P('dp', 'ctx')
- value_grad: bfloat16 [16, 2048, 512], P('dp', 'ctx')
- scale_grad: float32 [28], replicated
The draws below stay inside these ranges and needn't reach their ends.
Inputs may be any that keep to these rules, and one draw needn't show every extreme that they name: `routes`: each device's 128 slots hold its own 8 * 128 tokens of the sequence: the live slots come first, at least 16 of them, with positions rising along the sequence; -1 marks an empty slot; in every sequence the slots of some device are all live.
All inputs are finite; a program needn't handle non-finite values.
Results may differ from the reference program's by a relative error of at most 0.03.
Values may be sent and summed in bfloat16 or wider, within the bound.
No kernel may reach another device: no remote copies, remote signals or barrier semaphores. Data moves between devices by JAX's collectives and lax.ppermute only.
A program may use at most 64 MiB of HBM per device.

```python
import math
import jax
import jax.numpy as jnp
from jax import lax

QUERY_HEADS = 28
KEY_VALUE_HEADS = 4
HEAD_SIZE = 128
HEADS_PER_GROUP = 7
DEVICE_SLOTS = 128
SEQUENCE_SLOTS = 2048
SEQ_TOK = 16384
SEQUENCE_COUNT = 16


def draw_keys(key, part):
    key = jax.random.fold_in(key, 5)
    final_result = jnp.clip(jax.random.normal(jax.random.fold_in(key, 3), (SEQUENCE_COUNT, SEQUENCE_SLOTS, KEY_VALUE_HEADS * HEAD_SIZE), jnp.float32), -8.0, 8.0)
    return final_result.astype(jnp.bfloat16)


def draw_queries(key, part):
    key = jax.random.fold_in(key, 6)
    final_result = jnp.clip(jax.random.normal(jax.random.fold_in(key, 3), (SEQUENCE_COUNT, SEQUENCE_SLOTS, KEY_VALUE_HEADS * HEADS_PER_GROUP * HEAD_SIZE), jnp.float32), -8.0, 8.0)
    return final_result.astype(jnp.bfloat16)


def draw_routes(key, part):
    key = jax.random.fold_in(key, 9)
    stretches = SEQUENCE_SLOTS // DEVICE_SLOTS
    span = SEQ_TOK // stretches
    counts = jax.random.randint(jax.random.fold_in(key, 1), (SEQUENCE_COUNT, stretches), DEVICE_SLOTS // 8, DEVICE_SLOTS + 1)
    filled = jax.random.randint(jax.random.fold_in(key, 2), (SEQUENCE_COUNT, 1), 0, stretches)
    counts = jnp.where(jnp.arange(stretches)[None, :] == filled, DEVICE_SLOTS, counts)
    marks = jax.random.randint(jax.random.fold_in(key, 3), (SEQUENCE_COUNT, stretches, span), 0, 2 ** 20) * span + jnp.arange(span)[None, None, :]
    order = jnp.argsort(marks, axis=-1)[:, :, :DEVICE_SLOTS].astype(jnp.int32)
    live = jnp.arange(DEVICE_SLOTS)[None, None, :] < counts[:, :, None]
    picked = jnp.sort(jnp.where(live, order, span), axis=-1)
    offset = (jnp.arange(stretches) * span)[None, :, None]
    final_result = jnp.where(picked < span, picked + offset, -1)
    return final_result.reshape(SEQUENCE_COUNT, SEQUENCE_SLOTS).astype(jnp.int32)


def steps_of(key, dims, pieces, low, top_value):
    loudness, own = 1.0, jax.random.fold_in(key, 6)
    for dim, shards_of in pieces:
        heights = jnp.exp(jax.random.uniform(jax.random.fold_in(own, dim), (shards_of,), jnp.float32, low / len(pieces), top_value / len(pieces)))
        loudness = loudness * jnp.repeat(heights, dims[dim] // shards_of).reshape([-1 if axis == dim else 1 for axis in range(len(dims))])
    return loudness


def bell_draw(rng, extent, scale, limit, cuts=(), held_as=jnp.bfloat16):
    factor_of = steps_of(rng, extent, cuts, -0.22, 0.18) if cuts else 1.0
    drawn = jax.random.normal(rng, extent, jnp.float32) * scale * factor_of
    return jnp.minimum(jnp.maximum(drawn, -limit), limit).astype(held_as)


def setup_inputs(seed: int = 0) -> dict:
    key_list = jax.random.split(jax.random.key(seed), 7)
    queries = draw_queries(jax.random.fold_in(key_list[6], 71), 0)
    keys = draw_keys(jax.random.fold_in(key_list[6], 71), 0)
    values = bell_draw(key_list[2], (SEQUENCE_COUNT, SEQUENCE_SLOTS, KEY_VALUE_HEADS * HEAD_SIZE), 1.0, 6.0, ((0, 16), (1, 16)))
    out_grad = bell_draw(key_list[3], (SEQUENCE_COUNT, SEQUENCE_SLOTS, QUERY_HEADS * HEAD_SIZE), 1.0, 6.0, ((0, 16), (1, 16)))
    routes = draw_routes(jax.random.fold_in(key_list[6], 71), 0)
    per_head_scale = jnp.clip(jnp.exp(jax.random.uniform(key_list[5], (QUERY_HEADS,), jnp.float32, math.log(0.5), math.log(2.0))), 0.5, 2.0)
    return {"queries": queries, "keys": keys, "values": values, "out_grad": out_grad, "routes": routes, "per_head_scale": per_head_scale}


def reference(queries, keys, values, out_grad, routes, per_head_scale):
    shrink = 1.0 / math.sqrt(HEAD_SIZE)
    fourfold_scale = per_head_scale.astype(jnp.float32).reshape(KEY_VALUE_HEADS, HEADS_PER_GROUP, 1, 1)

    def one_sequence(items):
        query_all, key_every_slot, value_every_slot, grad_all, position = items
        key_head_rows = key_every_slot.astype(jnp.float32).reshape(SEQUENCE_SLOTS, KEY_VALUE_HEADS, HEAD_SIZE)
        value_head_rows = value_every_slot.astype(jnp.float32).reshape(SEQUENCE_SLOTS, KEY_VALUE_HEADS, HEAD_SIZE)

        def one_block(carry, block):
            key_gradient_sum, value_gradient_sum, scale_part = carry
            query_row_block, gradient_block, query_pos = block
            query_head_rows = query_row_block.astype(jnp.float32).reshape(DEVICE_SLOTS, KEY_VALUE_HEADS, HEADS_PER_GROUP, HEAD_SIZE)
            gradient_heads = gradient_block.astype(jnp.float32).reshape(DEVICE_SLOTS, KEY_VALUE_HEADS, HEADS_PER_GROUP, HEAD_SIZE)
            raw = jnp.einsum('qgha,kga->ghqk', query_head_rows, key_head_rows) * shrink
            scores = raw * fourfold_scale
            mask = (query_pos[:, None] >= 0) & (position[None, :] >= 0) & (position[None, :] <= query_pos[:, None])
            top = lax.optimization_barrier(jnp.max(jnp.where(mask, scores, -1e+30), axis=-1))
            total = lax.optimization_barrier(jnp.sum(jnp.where(mask, jnp.exp(scores - top[..., None]), 0.0), axis=-1))
            live = query_pos >= 0
            log_total = jnp.where(live, top + jnp.log(jnp.where(live, total, 1.0)), 0.0)
            dots = jnp.einsum('qgha,kga->ghqk', gradient_heads, value_head_rows)
            prob = jnp.where(mask, jnp.exp(scores - log_total[..., None]), 0.0)
            mean_dot = lax.optimization_barrier(jnp.sum(prob * dots, axis=-1))
            score_grad = prob * (dots - mean_dot[..., None])
            probability_lowered = lax.optimization_barrier(prob.astype(jnp.bfloat16))
            score_lowered = lax.optimization_barrier((score_grad * fourfold_scale * shrink).astype(jnp.bfloat16))
            query_grad = jnp.einsum('ghqk,kga->qgha', score_lowered.astype(jnp.float32), key_head_rows)
            key_gradient_sum = key_gradient_sum + jnp.einsum('pnmc,mpnl->cpl', score_lowered.astype(jnp.float32), query_head_rows).reshape(SEQUENCE_SLOTS, KEY_VALUE_HEADS * HEAD_SIZE)
            value_gradient_sum = value_gradient_sum + jnp.einsum('pnmc,mpnl->cpl', probability_lowered.astype(jnp.float32), gradient_heads).reshape(SEQUENCE_SLOTS, KEY_VALUE_HEADS * HEAD_SIZE)
            scale_part = scale_part + lax.optimization_barrier(jnp.sum(score_grad * raw, axis=(2, 3))).reshape(QUERY_HEADS)
            return ((key_gradient_sum, value_gradient_sum, scale_part), query_grad.reshape(DEVICE_SLOTS, QUERY_HEADS * HEAD_SIZE).astype(jnp.bfloat16))
        blocks = (query_all.reshape(SEQUENCE_SLOTS // DEVICE_SLOTS, DEVICE_SLOTS, QUERY_HEADS * HEAD_SIZE), grad_all.reshape(SEQUENCE_SLOTS // DEVICE_SLOTS, DEVICE_SLOTS, QUERY_HEADS * HEAD_SIZE), position.reshape(SEQUENCE_SLOTS // DEVICE_SLOTS, DEVICE_SLOTS))
        start_offset = (jnp.zeros((SEQUENCE_SLOTS, KEY_VALUE_HEADS * HEAD_SIZE), jnp.float32), jnp.zeros((SEQUENCE_SLOTS, KEY_VALUE_HEADS * HEAD_SIZE), jnp.float32), jnp.zeros((QUERY_HEADS,), jnp.float32))
        (key_gradient_sum, value_gradient_sum, scale_part), query_grad = lax.scan(one_block, start_offset, blocks)
        return (query_grad.reshape(SEQUENCE_SLOTS, QUERY_HEADS * HEAD_SIZE), key_gradient_sum.astype(jnp.bfloat16), value_gradient_sum.astype(jnp.bfloat16), scale_part)
    query_grad, key_grad, value_grad, scale_parts = lax.map(one_sequence, (queries, keys, values, out_grad, routes))
    return (query_grad, key_grad, value_grad, lax.optimization_barrier(jnp.sum(scale_parts, axis=0)))
```

```python
import functools
import math

import jax
import jax.numpy as jnp
from jax import lax
from jax.experimental import pallas as pl
from jax.experimental.pallas import tpu as pltpu
from jax.sharding import PartitionSpec as P

F32 = jnp.float32
BF16 = jnp.bfloat16
HEAD = 128
ROWS = 128
KV_HEADS = 2
GROUP = 7
HEADS = KV_HEADS * GROUP
WIDE = GROUP * ROWS
POS = 16
MESSAGE = POS + 2 * ROWS
TILE = 128
FAR = 32768.0
LOW = -1e30
LOG2E = 1.4426950408889634
NT = (((1,), (1,)), ((), ()))
NN = (((1,), (0,)), ((), ()))
TN = (((0,), (0,)), ((), ()))


def product(a, b, dims):
    return lax.dot_general(a, b, dims, preferred_element_type=F32)


def call(body, outs, scratch, flops, moved, operands):
    return pl.pallas_call(
        body,
        out_shape=outs,
        in_specs=operands,
        scratch_shapes=scratch,
        cost_estimate=pl.CostEstimate(
            flops=flops, bytes_accessed=moved, transcendentals=flops // 1024
        ),
        compiler_params=pltpu.CompilerParams(vmem_limit_bytes=48 * 1024 * 1024),
    )


def pack_keys_body(x_ref, key_ref, value_ref, pos_ref, keep_ref, send_ref):
    x = x_ref[0]
    pos = pos_ref[...]
    dead = pos < 0
    high = jnp.where(dead, 256, pos >> 7)
    low = jnp.where(dead, 0, pos & 127)
    row = jnp.concatenate([high, low], axis=1).astype(F32)
    rows = jnp.broadcast_to(row, (POS, 2 * ROWS)).astype(BF16)
    for ref, half in ((keep_ref, x), (send_ref, 1 - x)):
        at = pl.multiple_of(half * KV_HEADS * HEAD, KV_HEADS * HEAD)
        ref[0:POS, :] = rows
        ref[POS : POS + ROWS, :] = key_ref[:, pl.ds(at, KV_HEADS * HEAD)]
        ref[POS + ROWS : MESSAGE, :] = value_ref[:, pl.ds(at, KV_HEADS * HEAD)]


def pack_queries_body(x_ref, query_ref, grad_ref, keep_ref, send_ref):
    x = x_ref[0]
    for ref, half in ((keep_ref, x), (send_ref, 1 - x)):
        for number, source in enumerate((query_ref, grad_ref)):
            for head in range(HEADS):
                at = pl.multiple_of(half * HEADS * HEAD + head * HEAD, HEAD)
                ref[number, head * ROWS : (head + 1) * ROWS, :] = source[:, pl.ds(at, HEAD)]


def unpack_queries_body(x_ref, keep_ref, got_ref, out_ref):
    x = x_ref[0]
    for ref, half in ((keep_ref, x), (got_ref, 1 - x)):
        for head in range(HEADS):
            at = pl.multiple_of(half * HEADS * HEAD + head * HEAD, HEAD)
            out_ref[:, pl.ds(at, HEAD)] = ref[head * ROWS : (head + 1) * ROWS, :]


def positions(ref, slot):
    row = ref[slot, 0:POS, :].astype(F32)[0:1, :]
    return row[:, :ROWS] * 128.0 + row[:, ROWS:]


def query_side(own_ref):
    rows = [positions(own_ref, slot) for slot in range(2)]
    rows = [jnp.where(row >= FAR, -1.0, row) for row in rows]
    tops = [jnp.max(row) for row in rows]
    first = jnp.where(tops[0] < tops[1], 0, 1)
    return rows, tops, first


def place(blocks, first, top, key_c, value_c, pos_c, turned):
    key_c[...] = jnp.zeros_like(key_c)
    value_c[...] = jnp.zeros_like(value_c)
    pos_c[...] = jnp.full_like(pos_c, 1e9)
    start = jnp.int32(0)
    entries = []
    for phase in range(2):
        slot = first if phase == 0 else 1 - first
        rows = [positions(ref, slot) for ref in blocks]
        begins = [jnp.min(row) for row in rows]
        counts = [jnp.sum(jnp.where(row < FAR, 1.0, 0.0)).astype(jnp.int32) for row in rows]
        counts = [jnp.where(begin <= top, n, 0) for begin, n in zip(begins, counts)]
        spans = [(n + 15) >> 4 for n in counts]
        if len(blocks) == 2:
            ahead = begins[0] < begins[1]
            starts = [
                start + jnp.where(ahead, 0, spans[1] * 16),
                start + jnp.where(ahead, spans[0] * 16, 0),
            ]
        else:
            starts = []
            total = start
            for span in spans:
                starts.append(total)
                total = total + span * 16
        for ref, row, at, span in zip(blocks, rows, starts, spans):
            turned[...] = jnp.broadcast_to(row, (ROWS, ROWS)).T

            def chunk(step, _, ref=ref, at=at, slot=slot):
                source = pl.multiple_of(step * 16, 16)
                target = pl.multiple_of(at + step * 16, 16)
                pos_c[pl.ds(target, 16), :] = turned[pl.ds(source, 16), :]
                for g in range(KV_HEADS):
                    lanes = slice(g * HEAD, (g + 1) * HEAD)
                    key_c[g, pl.ds(target, 16), :] = ref[slot, pl.ds(POS + source, 16), lanes]
                    value_c[g, pl.ds(target, 16), :] = ref[
                        slot, pl.ds(POS + ROWS + source, 16), lanes
                    ]
                return 0

            lax.fori_loop(0, span, chunk, 0)
        entries.append((slot, starts, counts))
        start = start + sum(spans) * 16
    return start, entries


def stats_body(count, is_first, is_last, *refs):
    rate_ref, own_ref, kept_ref, got_ref = refs[:4]
    blocks = refs[4 : 4 + count]
    refs = refs[4 + count :]
    if not is_first:
        prior_ref, refs = refs[0], refs[1:]
    if is_last:
        final_ref, scale_ref, state, key_c, value_c, pos_c, turned = refs
    else:
        state, key_c, value_c, pos_c, turned = refs
    query_rows, tops, first = query_side(own_ref)
    length, _ = place(
        blocks, first, jnp.maximum(tops[0], tops[1]), key_c, value_c, pos_c, turned
    )
    if is_first:
        state[...] = jnp.zeros_like(state)
        state[:, 0:1, :] = jnp.full((2 * KV_HEADS, 1, WIDE), LOW, F32)
    else:
        state[...] = prior_ref[...]

    def tile(step, _):
        at = pl.multiple_of(step * TILE, TILE)
        key_pos = pos_c[pl.ds(at, TILE), :]
        lowest = jnp.min(key_pos)
        for slot in range(2):
            work_ref = (kept_ref, got_ref)[slot]

            @pl.when(lowest <= tops[slot])
            def _(slot=slot, work_ref=work_ref):
                mask = key_pos <= query_rows[slot]

                def group(g, _):
                    some = pl.ds(pl.multiple_of(g * WIDE, WIDE), WIDE)
                    keys = key_c[g, pl.ds(at, TILE), :]
                    values = value_c[g, pl.ds(at, TILE), :]
                    raw = product(keys, work_ref[0, some, :], NT)
                    dots = product(values, work_ref[1, some, :], NT)
                    for head in range(GROUP):
                        lanes = slice(head * ROWS, (head + 1) * ROWS)
                        scores = jnp.where(
                            mask, raw[:, lanes] * rate_ref[g, 0:1, lanes], LOW
                        )
                        held = state[slot * KV_HEADS + g, :, lanes]
                        top, total, weighted = held[0:1], held[1:2], held[2:3]
                        shifted, both = held[3:4], held[4:5]
                        new_top = jnp.maximum(top, jnp.max(scores, axis=0, keepdims=True))
                        above = scores - new_top
                        weights = jnp.exp2(above)
                        weighted_dots = weights * dots[:, lanes]
                        step_down = top - new_top
                        factor = jnp.exp2(step_down)
                        shifted = factor * (shifted + step_down * total) + jnp.sum(
                            weights * above, axis=0, keepdims=True
                        )
                        both = factor * (both + step_down * weighted) + jnp.sum(
                            weighted_dots * above, axis=0, keepdims=True
                        )
                        total = factor * total + jnp.sum(weights, axis=0, keepdims=True)
                        weighted = factor * weighted + jnp.sum(
                            weighted_dots, axis=0, keepdims=True
                        )
                        state[slot * KV_HEADS + g, 0:5, lanes] = jnp.concatenate(
                            [new_top, total, weighted, shifted, both], axis=0
                        )
                    return 0

                lax.fori_loop(0, KV_HEADS, group, 0)

        return 0

    lax.fori_loop(0, (length + TILE - 1) // TILE, tile, 0)
    if not is_last:
        return
    lane = lax.broadcasted_iota(jnp.int32, (8, ROWS), 1)
    scale_row = jnp.zeros((8, ROWS), F32)
    for slot in range(2):
        live = query_rows[slot] >= 0.0
        for g in range(KV_HEADS):
            for head in range(GROUP):
                lanes = slice(head * ROWS, (head + 1) * ROWS)
                held = state[slot * KV_HEADS + g, :, lanes]
                top, total, weighted = held[0:1], held[1:2], held[2:3]
                shifted, both = held[3:4], held[4:5]
                total = jnp.where(live, total, 1.0)
                mean = weighted / total
                spread = (both - mean * shifted) / total
                rate = rate_ref[g, 0:1, lanes] * math.sqrt(HEAD)
                spread = jnp.where(live, spread / rate, 0.0)
                final_ref[slot * KV_HEADS + g, 0:2, lanes] = jnp.concatenate(
                    [
                        jnp.where(live, top + jnp.log2(total), -LOW),
                        jnp.where(live, mean, 0.0),
                    ],
                    axis=0,
                )
                place_at = first * HEADS + g * GROUP + head
                scale_row = scale_row + jnp.where(
                    lane == place_at, jnp.sum(spread, axis=1, keepdims=True), 0.0
                )
    scale_ref[...] = scale_row


def grads_body(count, is_first, is_last, *refs):
    rate_ref, own_ref, kept_ref, got_ref, final_ref = refs[:5]
    blocks = refs[5 : 5 + count]
    refs = refs[5 + count :]
    if not is_first:
        prior_ref, refs = refs[0], refs[1:]
    outs, refs = refs[:count], refs[count:]
    if is_last:
        query_outs, refs = refs[:2], refs[2:]
    query_sum, key_c, value_c, pos_c, turned, key_sum, value_sum = refs
    query_rows, tops, first = query_side(own_ref)
    length, entries = place(
        blocks, first, jnp.maximum(tops[0], tops[1]), key_c, value_c, pos_c, turned
    )
    key_sum[...] = jnp.zeros_like(key_sum)
    value_sum[...] = jnp.zeros_like(value_sum)
    if is_first:
        query_sum[...] = jnp.zeros_like(query_sum)
    else:
        query_sum[...] = prior_ref[...]

    def tile(step, _):
        at = pl.multiple_of(step * TILE, TILE)
        key_pos = pos_c[pl.ds(at, TILE), :]
        lowest = jnp.min(key_pos)
        for slot in range(2):
            work_ref = (kept_ref, got_ref)[slot]

            @pl.when(lowest <= tops[slot])
            def _(slot=slot, work_ref=work_ref):
                mask = key_pos <= query_rows[slot]

                def group(g, _):
                    some = pl.ds(pl.multiple_of(g * WIDE, WIDE), WIDE)
                    keys = key_c[g, pl.ds(at, TILE), :]
                    values = value_c[g, pl.ds(at, TILE), :]
                    queries = work_ref[0, some, :]
                    gradients = work_ref[1, some, :]
                    raw = product(keys, queries, NT)
                    dots = product(values, gradients, NT)
                    probs, score_grads = [], []
                    for head in range(GROUP):
                        lanes = slice(head * ROWS, (head + 1) * ROWS)
                        rate = rate_ref[g, 0:1, lanes]
                        held = final_ref[slot * KV_HEADS + g, :, lanes]
                        prob = jnp.where(
                            mask, jnp.exp2(raw[:, lanes] * rate - held[0:1]), 0.0
                        )
                        grad = prob * (dots[:, lanes] - held[1:2])
                        probs.append(prob.astype(BF16))
                        score_grads.append((grad * (rate * (1.0 / LOG2E))).astype(BF16))
                    prob_low = jnp.concatenate(probs, axis=1)
                    score_low = jnp.concatenate(score_grads, axis=1)
                    rows = pl.ds(at, TILE)
                    value_sum[g, rows, :] += product(prob_low, gradients, NN)
                    key_sum[g, rows, :] += product(score_low, queries, NN)
                    query_sum[slot * KV_HEADS + g] += product(keys, score_low, TN)
                    return 0

                lax.fori_loop(0, KV_HEADS, group, 0)

        return 0

    lax.fori_loop(0, (length + TILE - 1) // TILE, tile, 0)
    row = lax.broadcasted_iota(jnp.int32, (ROWS, HEAD), 0)
    for slot, starts, counts in entries:
        for out, at, n in zip(outs, starts, counts):
            at = pl.multiple_of(at, 16)
            for g in range(KV_HEADS):
                lanes = slice(g * HEAD, (g + 1) * HEAD)
                for number, total in enumerate((key_sum, value_sum)):
                    out[slot, number * ROWS : (number + 1) * ROWS, lanes] = jnp.where(
                        row < n, total[g, pl.ds(at, ROWS), :], 0.0
                    )
    if is_last:
        for slot in range(2):
            for g in range(KV_HEADS):
                for head in range(GROUP):
                    lanes = slice(head * ROWS, (head + 1) * ROWS)
                    rows = slice((g * GROUP + head) * ROWS, (g * GROUP + head + 1) * ROWS)
                    query_outs[slot][rows, :] = query_sum[slot * KV_HEADS + g, :, lanes].T.astype(
                        BF16
                    )


def compact_scratch(count):
    size = (2 * count + 1) * ROWS
    return [
        pltpu.VMEM((KV_HEADS, size, HEAD), BF16),
        pltpu.VMEM((KV_HEADS, size, HEAD), BF16),
        pltpu.VMEM((size, ROWS), F32),
        pltpu.VMEM((ROWS, ROWS), F32),
    ]


STATE = jax.ShapeDtypeStruct((2 * KV_HEADS, 8, WIDE), F32)


def stats(rate, own, kept, got, blocks, prior=None, is_last=False):
    count = len(blocks)
    if is_last:
        outs = [STATE, jax.ShapeDtypeStruct((8, ROWS), F32)]
        scratch = [pltpu.VMEM(STATE.shape, F32)]
    else:
        outs, scratch = [STATE], []
    operands = [rate, own, kept, got, *blocks] + ([] if prior is None else [prior])
    return call(
        functools.partial(stats_body, count, prior is None, is_last),
        outs,
        scratch + compact_scratch(count),
        count * 2 * ROWS * 2 * HEADS * ROWS * 2 * HEAD * 2,
        4 << 20,
        [pl.BlockSpec(memory_space=pltpu.VMEM)] * len(operands),
    )(*operands)


def grads(rate, own, kept, got, final, blocks, prior=None, is_last=False):
    count = len(blocks)
    outs = [jax.ShapeDtypeStruct((2, 2 * ROWS, KV_HEADS * HEAD), F32)] * count
    sums = jax.ShapeDtypeStruct((2 * KV_HEADS, HEAD, WIDE), F32)
    operands = [rate, own, kept, got, final, *blocks] + ([] if prior is None else [prior])
    if is_last:
        outs = outs + [jax.ShapeDtypeStruct((HEADS * ROWS, HEAD), BF16)] * 2
        scratch = [pltpu.VMEM(sums.shape, F32)]
    else:
        outs, scratch = outs + [sums], []
    size = (2 * count + 1) * ROWS
    scratch = (
        scratch
        + compact_scratch(count)
        + [pltpu.VMEM((KV_HEADS, size, HEAD), F32), pltpu.VMEM((KV_HEADS, size, HEAD), F32)]
    )
    return call(
        functools.partial(grads_body, count, prior is None, is_last),
        outs,
        scratch,
        count * 2 * ROWS * 2 * HEADS * ROWS * 2 * HEAD * 5,
        6 << 20,
        [pl.BlockSpec(memory_space=pltpu.VMEM)] * len(operands),
    )(*operands)


def local(queries, keys, values, out_grad, routes, per_head_scale):
    me = lax.axis_index("ctx")
    size = lax.axis_size("ctx")
    ring = size // 2
    x = (me // ring).astype(jnp.int32)
    x_ref = x.reshape(1)
    across = [(i, (i + ring) % size) for i in range(size)]

    def neighbour(i, up):
        base, z = i // ring * ring, i % ring
        return base + (z + (1 if up == (z % 2 == 0) else -1)) % ring

    even = [(i, neighbour(i, True)) for i in range(size)]
    odd = [(i, neighbour(i, False)) for i in range(size)]

    def swap(array, pairs, axis="ctx"):
        return lax.ppermute(array, axis, pairs)

    smem = pl.BlockSpec(memory_space=pltpu.SMEM)
    vmem = pl.BlockSpec(memory_space=pltpu.VMEM)
    message = jax.ShapeDtypeStruct((MESSAGE, KV_HEADS * HEAD), BF16)
    keys_kept, keys_sent = call(
        pack_keys_body,
        [message, message],
        [],
        1024,
        1 << 20,
        operands=[smem, vmem, vmem, vmem],
    )(x_ref, keys[0], values[0], routes)
    keys_got = swap(keys_sent, across)
    work = jax.ShapeDtypeStruct((2, HEADS * ROWS, HEAD), BF16)
    kept, sent = call(
        pack_queries_body, [work, work], [], 1024, 4 << 20, operands=[smem, vmem, vmem]
    )(x_ref, queries[0], out_grad[0])
    got = swap(sent, across)
    own = jnp.stack([keys_kept, keys_got])

    half_scale = lax.dynamic_slice_in_dim(per_head_scale, x * HEADS, HEADS)
    rate = jnp.repeat(half_scale * (LOG2E / math.sqrt(HEAD)), ROWS).reshape(KV_HEADS, 1, WIDE)
    rate = jnp.broadcast_to(rate, (KV_HEADS, 8, WIDE))

    a, b = [own], [own]
    for step in range(1, 4):
        a.append(swap(b[step - 1], even))
        b.append(swap(a[step - 1], odd))
    a.append(swap(b[3], even))

    (state,) = stats(rate, own, kept, got, [own, a[1], b[1], a[2], b[2]])
    final, scale_part = stats(rate, own, kept, got, [a[3], b[3], a[4]], state, is_last=True)

    def exchange_sum(array):
        for bit in range(4):
            pairs = [(i, i ^ (1 << bit)) for i in range(16)]
            array = array + swap(array, pairs, "ctx")
        for bit in range(4):
            pairs = [(i, i ^ (1 << bit)) for i in range(16)]
            array = array + swap(array, pairs, "dp")
        return array

    scale_total = exchange_sum(scale_part)

    far, sums = grads(rate, own, kept, got, final, [a[4]])
    from_even = swap(far.astype(BF16), even)
    part_a, part_b, sums = grads(rate, own, kept, got, final, [a[3], b[3]], sums)
    sent_a = swap(part_a.astype(BF16), even)
    to_b = (part_b + from_even).astype(BF16)
    sent_b = swap(to_b, odd)
    for step in (2, 1):
        if step == 2:
            part_a, part_b, sums = grads(rate, own, kept, got, final, [a[2], b[2]], sums)
        else:
            near, sums = grads(rate, own, kept, got, final, [own], sums)
            part_a, part_b, query_kept, query_sent = grads(
                rate, own, kept, got, final, [a[1], b[1]], sums, is_last=True
            )
        to_a = (part_a + sent_b).astype(BF16)
        to_b = (part_b + sent_a).astype(BF16)
        sent_a, sent_b = swap(to_a, even), swap(to_b, odd)
    query_got = swap(query_sent, across)
    total = (near + sent_a + sent_b).astype(BF16)
    other = swap(total[1], across)
    left = jnp.where(x == 0, total[0], other)
    right = jnp.where(x == 0, other, total[0])
    both = jnp.concatenate([left, right], axis=1)
    query_out = call(
        unpack_queries_body,
        jax.ShapeDtypeStruct((ROWS, 2 * HEADS * HEAD), BF16),
        [],
        1024,
        2 << 20,
        operands=[smem, vmem, vmem],
    )(x_ref, query_kept, query_got)
    return (
        query_out[None],
        both[None, :ROWS],
        both[None, ROWS:],
        scale_total[0, : 2 * HEADS],
    )


def solution(mesh):
    in_specs = (
        P("dp", "ctx", None),
        P("dp", "ctx", None),
        P("dp", "ctx", None),
        P("dp", "ctx", None),
        P("dp", "ctx"),
        P(),
    )
    out_specs = (P("dp", "ctx", None), P("dp", "ctx", None), P("dp", "ctx", None), P())
    return jax.shard_map(local, mesh=mesh, in_specs=in_specs, out_specs=out_specs, check_vma=False)
```

```python
import functools
import math

import jax
import jax.numpy as jnp
from jax import lax
from jax.experimental import pallas as pl
from jax.experimental.pallas import tpu as pltpu
from jax.sharding import PartitionSpec as P

F32 = jnp.float32
BF16 = jnp.bfloat16
HEAD = 128
ROWS = 128
KV_HEADS = 2
GROUP = 7
HEADS = KV_HEADS * GROUP
WIDE = GROUP * ROWS
POS = 16
MESSAGE = POS + 2 * ROWS
TILE = 128
FAR = 32768.0
LOW = -1e30
LOG2E = 1.4426950408889634
NT = (((1,), (1,)), ((), ()))
NN = (((1,), (0,)), ((), ()))
TN = (((0,), (0,)), ((), ()))


def product(a, b, dims):
    return lax.dot_general(a, b, dims, preferred_element_type=F32)


def call(body, outs, scratch, flops, moved, operands):
    return pl.pallas_call(
        body,
        out_shape=outs,
        in_specs=operands,
        scratch_shapes=scratch,
        cost_estimate=pl.CostEstimate(
            flops=flops, bytes_accessed=moved, transcendentals=flops // 1024
        ),
        compiler_params=pltpu.CompilerParams(vmem_limit_bytes=20 * 1024 * 1024),
    )


def fetch(sources, targets, sem):
    copies = [
        pltpu.make_async_copy(source, target, sem.at[n])
        for n, (source, target) in enumerate(zip(sources, targets))
    ]
    for copy in copies:
        copy.start()
    for copy in copies:
        copy.wait()


def pack_keys_body(x_ref, key_in, value_in, pos_in, keep_ref, send_ref, key_ref, value_ref, pos_ref, sem):
    x = x_ref[0]
    fetch((key_in, value_in, pos_in), (key_ref, value_ref, pos_ref), sem)
    pos = pos_ref[...]
    dead = pos < 0
    high = jnp.where(dead, 256, pos >> 7)
    low = jnp.where(dead, 0, pos & 127)
    row = jnp.concatenate([high, low], axis=1).astype(F32)
    rows = jnp.broadcast_to(row, (POS, 2 * ROWS)).astype(BF16)
    for ref, half in ((keep_ref, x), (send_ref, 1 - x)):
        at = pl.multiple_of(half * KV_HEADS * HEAD, KV_HEADS * HEAD)
        ref[0:POS, :] = rows
        ref[POS : POS + ROWS, :] = key_ref[:, pl.ds(at, KV_HEADS * HEAD)]
        ref[POS + ROWS : MESSAGE, :] = value_ref[:, pl.ds(at, KV_HEADS * HEAD)]


def pack_queries_body(x_ref, after_ref, query_in, grad_in, keep_ref, send_ref, query_ref, grad_ref, sem):
    x = x_ref[0]
    fetch((query_in, grad_in), (query_ref, grad_ref), sem)
    for ref, half in ((send_ref, 1 - x), (keep_ref, x)):
        for number, source in enumerate((query_ref, grad_ref)):
            for head in range(HEADS):
                at = pl.multiple_of(half * HEADS * HEAD + head * HEAD, HEAD)
                ref[number, head * ROWS : (head + 1) * ROWS, :] = source[:, pl.ds(at, HEAD)]


def join_body(after_ref, keep_ref, got_ref, out_ref):
    out_ref[0] = keep_ref[...]
    out_ref[1] = got_ref[...]


def finish_body(count, x_ref, keep_ref, got_ref, own_ref, other_ref, *refs):
    scale_refs = refs[:count]
    query_out, key_out, value_out, scale_out = refs[count:]
    x = x_ref[0]
    scale = sum([ref[0:1, :] for ref in scale_refs[1:]], scale_refs[0][0:1, :])
    scale_out[...] = scale[:, : 2 * HEADS]
    for ref, half in ((own_ref, x), (other_ref, 1 - x)):
        at = pl.multiple_of(half * KV_HEADS * HEAD, KV_HEADS * HEAD)
        key_out[:, pl.ds(at, KV_HEADS * HEAD)] = ref[:ROWS, :]
        value_out[:, pl.ds(at, KV_HEADS * HEAD)] = ref[ROWS:, :]
    for ref, half in ((keep_ref, x), (got_ref, 1 - x)):
        for head in range(HEADS):
            at = pl.multiple_of(half * HEADS * HEAD + head * HEAD, HEAD)
            query_out[:, pl.ds(at, HEAD)] = ref[head * ROWS : (head + 1) * ROWS, :]


def positions(ref, slot):
    row = ref[slot, 0:POS, :].astype(F32)[0:1, :]
    return row[:, :ROWS] * 128.0 + row[:, ROWS:]


def query_side(own_ref):
    rows = [positions(own_ref, slot) for slot in range(2)]
    rows = [jnp.where(row >= FAR, -1.0, row) for row in rows]
    tops = [jnp.max(row) for row in rows]
    first = jnp.where(tops[0] < tops[1], 0, 1)
    return rows, tops, first


def place(blocks, first, top, key_c, value_c, pos_c, turned):
    start = jnp.int32(0)
    entries = []
    for phase in range(2):
        slot = first if phase == 0 else 1 - first
        rows = [positions(ref, slot) for ref in blocks]
        begins = [jnp.min(row) for row in rows]
        counts = [jnp.sum(jnp.where(row < FAR, 1.0, 0.0)).astype(jnp.int32) for row in rows]
        counts = [jnp.where(begin <= top, n, 0) for begin, n in zip(begins, counts)]
        spans = [(n + 15) >> 4 for n in counts]
        if len(blocks) == 2:
            ahead = begins[0] < begins[1]
            starts = [
                start + jnp.where(ahead, 0, spans[1] * 16),
                start + jnp.where(ahead, spans[0] * 16, 0),
            ]
        else:
            starts = []
            total = start
            for span in spans:
                starts.append(total)
                total = total + span * 16
        for ref, row, at, span in zip(blocks, rows, starts, spans):
            turned[...] = jnp.broadcast_to(row, (ROWS, ROWS)).T

            def chunk(step, _, ref=ref, at=at, slot=slot):
                source = pl.multiple_of(step * 16, 16)
                target = pl.multiple_of(at + step * 16, 16)
                pos_c[pl.ds(target, 16), :] = turned[pl.ds(source, 16), :]
                for g in range(KV_HEADS):
                    lanes = slice(g * HEAD, (g + 1) * HEAD)
                    key_c[g, pl.ds(target, 16), :] = ref[slot, pl.ds(POS + source, 16), lanes]
                    value_c[g, pl.ds(target, 16), :] = ref[
                        slot, pl.ds(POS + ROWS + source, 16), lanes
                    ]
                return 0

            lax.fori_loop(0, span, chunk, 0)
        entries.append((slot, starts, counts))
        start = start + sum(spans) * 16
    rest = pl.ds(pl.multiple_of(start, 16), TILE)
    pos_c[rest, :] = jnp.full((TILE, ROWS), 1e9, F32)
    for g in range(KV_HEADS):
        key_c[g, rest, :] = jnp.zeros((TILE, HEAD), BF16)
        value_c[g, rest, :] = jnp.zeros((TILE, HEAD), BF16)
    return start, entries


def stats_tile(rate_ref, work_ref, state, key_c, value_c, mask, at, slot, g):
    some = slice(g * WIDE, (g + 1) * WIDE)
    raw = product(key_c[g, pl.ds(at, TILE), :], work_ref[0, some, :], NT)
    dots = product(value_c[g, pl.ds(at, TILE), :], work_ref[1, some, :], NT)
    for head in range(GROUP):
        lanes = slice(head * ROWS, (head + 1) * ROWS)
        scores = jnp.where(mask, raw[:, lanes] * rate_ref[g, 0:1, lanes], LOW)
        held = [state[slot * KV_HEADS + g, n, :, lanes] for n in range(5)]
        top, total, weighted, shifted, both = held
        scores = scores.reshape(TILE // 8, 8, ROWS)
        new_top = jnp.maximum(top, jnp.max(scores, axis=0))
        above = scores - new_top[None]
        weights = jnp.exp2(above)
        weighted_dots = weights * dots[:, lanes].reshape(TILE // 8, 8, ROWS)
        step_down = top - new_top
        factor = jnp.exp2(step_down)
        held = [
            new_top,
            factor * total + jnp.sum(weights, axis=0),
            factor * weighted + jnp.sum(weighted_dots, axis=0),
            factor * (shifted + step_down * total) + jnp.sum(weights * above, axis=0),
            factor * (both + step_down * weighted) + jnp.sum(weighted_dots * above, axis=0),
        ]
        for n in range(5):
            state[slot * KV_HEADS + g, n, :, lanes] = held[n]


def stats_body(jobs, is_first, is_last, *refs):
    rate_ref, own_ref, kept_ref, got_ref = refs[:4]
    refs = refs[4:]
    work = []
    for count, slots in jobs:
        work.append((refs[:count], slots))
        refs = refs[count:]
    if not is_first:
        prior_ref, refs = refs[0], refs[1:]
    if is_last:
        final_ref, scale_ref, state, key_c, value_c, pos_c, turned = refs
    else:
        state, key_c, value_c, pos_c, turned = refs
    query_rows, tops, first = query_side(own_ref)
    if is_first:
        state[...] = jnp.zeros_like(state)
        state[:, 0] = jnp.full((2 * KV_HEADS, 8, WIDE), LOW, F32)
    else:
        state[...] = prior_ref[...]
    for blocks, slots in work:
        top = jnp.maximum(tops[0], tops[1]) if len(slots) == 2 else tops[slots[0]]
        length, _ = place(blocks, first, top, key_c, value_c, pos_c, turned)

        def tile(step, _, slots=slots):
            at = pl.multiple_of(step * TILE, TILE)
            key_pos = pos_c[pl.ds(at, TILE), :]
            lowest = jnp.min(key_pos)
            for slot in slots:

                @pl.when(lowest <= tops[slot])
                def _(slot=slot):
                    mask = key_pos <= query_rows[slot]
                    for g in range(KV_HEADS):
                        stats_tile(
                            rate_ref, (kept_ref, got_ref)[slot], state, key_c, value_c, mask, at, slot, g
                        )

            return 0

        lax.fori_loop(0, (length + TILE - 1) // TILE, tile, 0)
    if not is_last:
        return
    lane = lax.broadcasted_iota(jnp.int32, (8, ROWS), 1)
    scale_row = jnp.zeros((8, ROWS), F32)
    for slot in range(2):
        live = query_rows[slot] >= 0.0
        for g in range(KV_HEADS):
            for head in range(GROUP):
                lanes = slice(head * ROWS, (head + 1) * ROWS)
                held = [state[slot * KV_HEADS + g, n, :, lanes] for n in range(5)]
                tops_in, total, weighted, shifted, both = held
                top = jnp.max(tops_in, axis=0, keepdims=True)
                step_down = tops_in - top
                factor = jnp.exp2(step_down)
                both = jnp.sum(factor * (both + step_down * weighted), axis=0, keepdims=True)
                shifted = jnp.sum(factor * (shifted + step_down * total), axis=0, keepdims=True)
                weighted = jnp.sum(factor * weighted, axis=0, keepdims=True)
                total = jnp.sum(factor * total, axis=0, keepdims=True)
                total = jnp.where(live, total, 1.0)
                mean = weighted / total
                spread = (both - mean * shifted) / total
                rate = rate_ref[g, 0:1, lanes] * math.sqrt(HEAD)
                spread = jnp.where(live, spread / rate, 0.0)
                final_ref[slot * KV_HEADS + g, 0:2, lanes] = jnp.concatenate(
                    [
                        jnp.where(live, top + jnp.log2(total), -LOW),
                        jnp.where(live, mean, 0.0),
                    ],
                    axis=0,
                )
                place_at = first * HEADS + g * GROUP + head
                scale_row = scale_row + jnp.where(
                    lane == place_at, jnp.sum(spread, axis=1, keepdims=True), 0.0
                )
    scale_ref[...] = scale_row


def grads_tile(
    rate_ref,
    work_ref,
    final_ref,
    key_c,
    value_c,
    key_sum,
    value_sum,
    query_sum,
    mask,
    at,
    slot,
    g,
):
    some = slice(g * WIDE, (g + 1) * WIDE)
    rows = pl.ds(at, TILE)
    keys = key_c[g, rows, :]
    values = value_c[g, rows, :]
    queries = work_ref[0, some, :]
    gradients = work_ref[1, some, :]
    raw = product(keys, queries, NT)
    dots = product(values, gradients, NT)
    probs, score_grads = [], []
    for head in range(GROUP):
        lanes = slice(head * ROWS, (head + 1) * ROWS)
        rate = rate_ref[g, 0:1, lanes]
        held = final_ref[slot * KV_HEADS + g, :, lanes]
        prob = jnp.where(mask, jnp.exp2(raw[:, lanes] * rate - held[0:1]), 0.0)
        grad = prob * (dots[:, lanes] - held[1:2])
        probs.append(prob.astype(BF16))
        score_grads.append((grad * (rate * (1.0 / LOG2E))).astype(BF16))
    prob_low = jnp.concatenate(probs, axis=1)
    score_low = jnp.concatenate(score_grads, axis=1)
    value_sum[g, rows, :] += product(prob_low, gradients, NN)
    key_sum[g, rows, :] += product(score_low, queries, NN)
    query_sum[slot * KV_HEADS + g] += product(keys, score_low, TN)


def grads_body(count, added, is_first, is_last, *refs):
    rate_ref, own_ref, kept_ref, got_ref, final_ref = refs[:5]
    blocks = refs[5 : 5 + count]
    refs = refs[5 + count :]
    scale_refs, refs = refs[:added], refs[added:]
    if not is_first:
        prior_ref, refs = refs[0], refs[1:]
    outs, refs = refs[:count], refs[count:]
    if added:
        scale_ref, refs = refs[0], refs[1:]
        scale_ref[...] = sum([ref[...] for ref in scale_refs[1:]], scale_refs[0][...])
    if is_last:
        query_outs, refs = refs[:2], refs[2:]
    query_sum, key_c, value_c, pos_c, turned, key_sum, value_sum = refs
    query_rows, tops, first = query_side(own_ref)
    length, entries = place(
        blocks, first, jnp.maximum(tops[0], tops[1]), key_c, value_c, pos_c, turned
    )
    if is_first:
        query_sum[...] = jnp.zeros_like(query_sum)
    else:
        query_sum[...] = prior_ref[...]

    def tile(step, _):
        at = pl.multiple_of(step * TILE, TILE)
        key_pos = pos_c[pl.ds(at, TILE), :]
        lowest = jnp.min(key_pos)
        for g in range(KV_HEADS):
            key_sum[g, pl.ds(at, TILE), :] = jnp.zeros((TILE, HEAD), F32)
            value_sum[g, pl.ds(at, TILE), :] = jnp.zeros((TILE, HEAD), F32)
        for slot in range(2):

            @pl.when(lowest <= tops[slot])
            def _(slot=slot):
                mask = key_pos <= query_rows[slot]
                for g in range(KV_HEADS):
                    grads_tile(
                        rate_ref,
                        (kept_ref, got_ref)[slot],
                        final_ref,
                        key_c,
                        value_c,
                        key_sum,
                        value_sum,
                        query_sum,
                        mask,
                        at,
                        slot,
                        g,
                    )

        return 0

    lax.fori_loop(0, (length + TILE - 1) // TILE, tile, 0)
    row = lax.broadcasted_iota(jnp.int32, (ROWS, HEAD), 0)
    for slot, starts, counts in entries:
        for out, at, n in zip(outs, starts, counts):
            at = pl.multiple_of(at, 16)
            for g in range(KV_HEADS):
                lanes = slice(g * HEAD, (g + 1) * HEAD)
                for number, total in enumerate((key_sum, value_sum)):
                    out[slot, number * ROWS : (number + 1) * ROWS, lanes] = jnp.where(
                        row < n, total[g, pl.ds(at, ROWS), :], 0.0
                    )
    if is_last:
        for slot in range(2):
            for g in range(KV_HEADS):
                for head in range(GROUP):
                    lanes = slice(head * ROWS, (head + 1) * ROWS)
                    rows = slice((g * GROUP + head) * ROWS, (g * GROUP + head + 1) * ROWS)
                    query_outs[slot][rows, :] = query_sum[slot * KV_HEADS + g, :, lanes].T.astype(
                        BF16
                    )


def compact_scratch(count):
    size = (2 * count + 1) * ROWS
    return [
        pltpu.VMEM((KV_HEADS, size, HEAD), BF16),
        pltpu.VMEM((KV_HEADS, size, HEAD), BF16),
        pltpu.VMEM((size, ROWS), F32),
        pltpu.VMEM((ROWS, ROWS), F32),
    ]


STATE = jax.ShapeDtypeStruct((2 * KV_HEADS, 5, 8, WIDE), F32)
FINAL = jax.ShapeDtypeStruct((2 * KV_HEADS, 8, WIDE), F32)


def stats(rate, own, kept, got, jobs, prior=None, is_last=False):
    if is_last:
        outs = [FINAL, jax.ShapeDtypeStruct((8, ROWS), F32)]
        scratch = [pltpu.VMEM(STATE.shape, F32)]
    else:
        outs, scratch = [STATE], []
    blocks = [block for some, _ in jobs for block in some]
    operands = [rate, own, kept, got, *blocks] + ([] if prior is None else [prior])
    sizes = [(len(some), slots) for some, slots in jobs]
    return call(
        functools.partial(stats_body, sizes, prior is None, is_last),
        outs,
        scratch + compact_scratch(max(count for count, _ in sizes)),
        sum(count * len(slots) for count, slots in sizes) * ROWS * 2 * HEADS * ROWS * HEAD * 4,
        4 << 20,
        [pl.BlockSpec(memory_space=pltpu.VMEM)] * len(operands),
    )(*operands)


def grads(rate, own, kept, got, final, blocks, scales=(), prior=None, is_last=False):
    count = len(blocks)
    outs = [jax.ShapeDtypeStruct((2, 2 * ROWS, KV_HEADS * HEAD), F32)] * count
    sums = jax.ShapeDtypeStruct((2 * KV_HEADS, HEAD, WIDE), F32)
    operands = [rate, own, kept, got, final, *blocks, *scales]
    operands = operands + ([] if prior is None else [prior])
    if scales:
        outs = outs + [jax.ShapeDtypeStruct((8, ROWS), F32)]
    if is_last:
        outs = outs + [jax.ShapeDtypeStruct((HEADS * ROWS, HEAD), BF16)] * 2
        scratch = [pltpu.VMEM(sums.shape, F32)]
    else:
        outs, scratch = outs + [sums], []
    size = (2 * count + 1) * ROWS
    scratch = (
        scratch
        + compact_scratch(count)
        + [pltpu.VMEM((KV_HEADS, size, HEAD), F32), pltpu.VMEM((KV_HEADS, size, HEAD), F32)]
    )
    return call(
        functools.partial(grads_body, count, len(scales), prior is None, is_last),
        outs,
        scratch,
        count * 2 * ROWS * 2 * HEADS * ROWS * 2 * HEAD * 5,
        6 << 20,
        [pl.BlockSpec(memory_space=pltpu.VMEM)] * len(operands),
    )(*operands)


def local(queries, keys, values, out_grad, routes, per_head_scale):
    me = lax.axis_index("ctx")
    size = lax.axis_size("ctx")
    ring = size // 2
    x = (me // ring).astype(jnp.int32)
    x_ref = x.reshape(1)
    across = [(i, (i + ring) % size) for i in range(size)]

    def neighbour(i, up):
        base, z = i // ring * ring, i % ring
        return base + (z + (1 if up == (z % 2 == 0) else -1)) % ring

    even = [(i, neighbour(i, True)) for i in range(size)]
    odd = [(i, neighbour(i, False)) for i in range(size)]

    def swap(array, pairs, axis="ctx"):
        return lax.ppermute(array, axis, pairs)

    smem = pl.BlockSpec(memory_space=pltpu.SMEM)
    vmem = pl.BlockSpec(memory_space=pltpu.VMEM)
    anywhere = pl.BlockSpec(memory_space=pl.ANY)
    width = KV_HEADS * HEAD
    message = jax.ShapeDtypeStruct((MESSAGE, width), BF16)
    keys_kept, keys_sent = call(
        pack_keys_body,
        [message, message],
        [
            pltpu.VMEM((ROWS, 2 * width), BF16),
            pltpu.VMEM((ROWS, 2 * width), BF16),
            pltpu.VMEM((1, ROWS), jnp.int32),
            pltpu.SemaphoreType.DMA((3,)),
        ],
        1024,
        1 << 20,
        [smem, anywhere, anywhere, anywhere],
    )(x_ref, keys[0], values[0], routes)
    keys_got = swap(keys_sent, across)
    work = jax.ShapeDtypeStruct((2, HEADS * ROWS, HEAD), BF16)
    kept, sent = call(
        pack_queries_body,
        [work, work],
        [
            pltpu.VMEM((ROWS, 2 * HEADS * HEAD), BF16),
            pltpu.VMEM((ROWS, 2 * HEADS * HEAD), BF16),
            pltpu.SemaphoreType.DMA((2,)),
        ],
        1024,
        4 << 20,
        [smem, anywhere, anywhere, anywhere],
    )(x_ref, keys_sent, queries[0], out_grad[0])
    got = swap(sent, across)
    own = call(
        join_body,
        jax.ShapeDtypeStruct((2, MESSAGE, width), BF16),
        [],
        1024,
        1 << 20,
        [anywhere, vmem, vmem],
    )(kept, keys_kept, keys_got)

    half_scale = lax.dynamic_slice_in_dim(per_head_scale, x * HEADS, HEADS)
    rate = jnp.repeat(half_scale * (LOG2E / math.sqrt(HEAD)), ROWS).reshape(KV_HEADS, 1, WIDE)
    rate = jnp.broadcast_to(rate, (KV_HEADS, 8, WIDE))

    a, b = [own], [own]
    for step in range(1, 4):
        a.append(swap(b[step - 1], even))
        b.append(swap(a[step - 1], odd))
    a.append(swap(b[3], even))

    (state,) = stats(rate, own, kept, kept, [([own, a[1], b[1]], (0,))])
    (state,) = stats(
        rate, own, kept, got, [([own, a[1], b[1]], (1,)), ([a[2], b[2]], (0, 1))], state
    )
    (state,) = stats(rate, own, kept, got, [([a[3], b[3]], (0, 1))], state)
    final, scale = stats(rate, own, kept, got, [([a[4]], (0, 1))], state, is_last=True)

    total_devices = lax.axis_size("dp") * size

    def exchange(array, masks):
        pairs = [[(i, i ^ mask) for i in range(total_devices)] for mask in masks]
        return [array] + [swap(array, pair, ("dp", "ctx")) for pair in pairs]

    scales = exchange(scale, (8,))
    far, sums = grads(rate, own, kept, got, final, [a[4]])
    from_even = swap(far.astype(BF16), even)
    part_a, part_b, scale, sums = grads(
        rate, own, kept, got, final, [a[3], b[3]], scales, sums
    )
    scales = exchange(scale, (16,))
    sent_a = swap(part_a.astype(BF16), even)
    sent_b = swap((part_b + from_even).astype(BF16), odd)
    part_a, part_b, near, scale, sums = grads(
        rate, own, kept, got, final, [a[2], b[2], own], scales, sums
    )
    scales = exchange(scale, (1, 2, 3))
    to_a = (part_a + sent_b).astype(BF16)
    to_b = (part_b + sent_a).astype(BF16)
    sent_a, sent_b = swap(to_a, even), swap(to_b, odd)
    part_a, part_b, scale, query_kept, query_sent = grads(
        rate, own, kept, got, final, [a[1], b[1]], scales, sums, is_last=True
    )
    query_got = swap(query_sent, across)
    scales = exchange(scale, (4, 32, 36))
    to_a = (part_a + sent_b).astype(BF16)
    to_b = (part_b + sent_a).astype(BF16)
    sent_a, sent_b = swap(to_a, even), swap(to_b, odd)
    scales = exchange(sum(scales[1:], scales[0]), (64, 128, 192))
    ours = (near[0] + sent_a[0] + sent_b[0]).astype(BF16)
    theirs = (near[1] + sent_a[1] + sent_b[1]).astype(BF16)
    other = swap(theirs, across)
    query_out, key_out, value_out, scale_out = call(
        functools.partial(finish_body, len(scales)),
        [
            jax.ShapeDtypeStruct((ROWS, 2 * HEADS * HEAD), BF16),
            jax.ShapeDtypeStruct((ROWS, 2 * width), BF16),
            jax.ShapeDtypeStruct((ROWS, 2 * width), BF16),
            jax.ShapeDtypeStruct((1, 2 * HEADS), F32),
        ],
        [],
        1024,
        2 << 20,
        [smem] + [vmem] * (4 + len(scales)),
    )(x_ref, query_kept, query_got, ours, other, *scales)
    return query_out[None], key_out[None], value_out[None], scale_out.reshape(2 * HEADS)


def solution(mesh):
    in_specs = (
        P("dp", "ctx", None),
        P("dp", "ctx", None),
        P("dp", "ctx", None),
        P("dp", "ctx", None),
        P("dp", "ctx"),
        P(),
    )
    out_specs = (P("dp", "ctx", None), P("dp", "ctx", None), P("dp", "ctx", None), P())
    return jax.shard_map(local, mesh=mesh, in_specs=in_specs, out_specs=out_specs, check_vma=False)
```

```python
import functools
import math

import jax
import jax.numpy as jnp
from jax import lax
from jax.experimental import pallas as pl
from jax.experimental.pallas import tpu as pltpu
from jax.sharding import PartitionSpec as P

F32 = jnp.float32
BF16 = jnp.bfloat16
HEAD = 128
ROWS = 128
KV_HEADS = 2
GROUP = 7
HEADS = KV_HEADS * GROUP
WIDE = GROUP * ROWS
POS = 16
MESSAGE = POS + 2 * ROWS
TILE = 128
FAR = 32768.0
LOW = -1e30
LOG2E = 1.4426950408889634
NT = (((1,), (1,)), ((), ()))
NN = (((1,), (0,)), ((), ()))
TN = (((0,), (0,)), ((), ()))


def product(a, b, dims):
    return lax.dot_general(a, b, dims, preferred_element_type=F32)


def call(body, outs, scratch, flops, moved, operands):
    return pl.pallas_call(
        body,
        out_shape=outs,
        in_specs=operands,
        scratch_shapes=scratch,
        cost_estimate=pl.CostEstimate(
            flops=flops, bytes_accessed=moved, transcendentals=flops // 1024
        ),
        compiler_params=pltpu.CompilerParams(vmem_limit_bytes=20 * 1024 * 1024),
    )


def fetch(sources, targets, sem):
    copies = [
        pltpu.make_async_copy(source, target, sem.at[n])
        for n, (source, target) in enumerate(zip(sources, targets))
    ]
    for copy in copies:
        copy.start()
    for copy in copies:
        copy.wait()


def pack_keys_body(x_ref, key_in, value_in, pos_in, keep_ref, send_ref, key_ref, value_ref, pos_ref, sem):
    x = x_ref[0]
    fetch((key_in, value_in, pos_in), (key_ref, value_ref, pos_ref), sem)
    pos = pos_ref[...]
    dead = pos < 0
    high = jnp.where(dead, 256, pos >> 7)
    low = jnp.where(dead, 0, pos & 127)
    row = jnp.concatenate([high, low], axis=1).astype(F32)
    rows = jnp.broadcast_to(row, (POS, 2 * ROWS)).astype(BF16)
    for ref, half in ((keep_ref, x), (send_ref, 1 - x)):
        at = pl.multiple_of(half * KV_HEADS * HEAD, KV_HEADS * HEAD)
        ref[0:POS, :] = rows
        ref[POS : POS + ROWS, :] = key_ref[:, pl.ds(at, KV_HEADS * HEAD)]
        ref[POS + ROWS : MESSAGE, :] = value_ref[:, pl.ds(at, KV_HEADS * HEAD)]


def pack_queries_body(x_ref, after_ref, query_in, grad_in, keep_ref, send_ref, query_ref, grad_ref, sem):
    x = x_ref[0]
    fetch((query_in, grad_in), (query_ref, grad_ref), sem)
    for ref, half in ((send_ref, 1 - x), (keep_ref, x)):
        for number, source in enumerate((query_ref, grad_ref)):
            for head in range(HEADS):
                at = pl.multiple_of(half * HEADS * HEAD + head * HEAD, HEAD)
                ref[number, head * ROWS : (head + 1) * ROWS, :] = source[:, pl.ds(at, HEAD)]


def join_body(after_ref, keep_ref, got_ref, out_ref):
    out_ref[0] = keep_ref[...]
    out_ref[1] = got_ref[...]


def finish_body(
    x_ref,
    keep_ref,
    got_ref,
    own_ref,
    other_ref,
    *refs,
):
    scale_refs, (query_out, key_out, value_out, scale_out) = refs[:4], refs[4:]
    x = x_ref[0]
    scale = four([ref[...] for ref in scale_refs])
    scale_out[...] = scale[0:1, : 2 * HEADS]
    for ref, half in ((own_ref, x), (other_ref, 1 - x)):
        at = pl.multiple_of(half * KV_HEADS * HEAD, KV_HEADS * HEAD)
        key_out[:, pl.ds(at, KV_HEADS * HEAD)] = ref[:ROWS, :]
        value_out[:, pl.ds(at, KV_HEADS * HEAD)] = ref[ROWS : 2 * ROWS, :]
    for ref, half in ((keep_ref, x), (got_ref, 1 - x)):
        for head in range(HEADS):
            at = pl.multiple_of(half * HEADS * HEAD + head * HEAD, HEAD)
            query_out[:, pl.ds(at, HEAD)] = ref[head * ROWS : (head + 1) * ROWS, :]


def positions(ref, slot):
    row = ref[slot, 0:POS, :].astype(F32)[0:1, :]
    return row[:, :ROWS] * 128.0 + row[:, ROWS:]


def query_side(own_ref):
    rows = [positions(own_ref, slot) for slot in range(2)]
    rows = [jnp.where(row >= FAR, -1.0, row) for row in rows]
    tops = [jnp.max(row) for row in rows]
    first = jnp.where(tops[0] < tops[1], 0, 1)
    return rows, tops, first


def four(parts):
    return (parts[0] + parts[1]) + (parts[2] + parts[3])


def code(value):
    high = value.astype(BF16)
    value = value - high.astype(F32)
    middle = value.astype(BF16)
    return [high, middle, (value - middle.astype(F32)).astype(BF16)]


def put_scale(ref, scale):
    for number, part in enumerate(code(scale)):
        lanes = slice(0, ROWS) if number < 2 else slice(ROWS, 2 * ROWS)
        rows = jnp.concatenate([part] * 2, axis=0)
        at = 2 * ROWS + (number % 2) * 16
        ref[at : at + 16, lanes] = rows
    ref[2 * ROWS + 16 : 2 * ROWS + 32, ROWS : 2 * ROWS] = jnp.zeros((16, ROWS), BF16)


def get_scale(ref):
    at = 2 * ROWS
    high = ref[at : at + 16, :ROWS].astype(F32)
    middle = ref[at + 16 : at + 32, :ROWS].astype(F32)
    low = ref[at : at + 16, ROWS:].astype(F32)
    return ((high + middle) + low)[0:8]


def hop_body(step, count, *refs):
    part_a, part_b, sent_a = refs[:3]
    refs = refs[3:]
    if step < 3:
        sent_b, refs = refs[0], refs[1:]
    scale_refs, (to_a, to_b, scale_out) = refs[:count], refs[count:]
    plain = slice(0, 2 * ROWS)
    for slot in range(2):
        first = part_a[slot]
        if step < 3:
            first = first + sent_b[slot, plain, :].astype(F32)
        to_a[slot, plain, :] = first.astype(BF16)
        second = part_b[slot] + sent_a[slot, plain, :].astype(F32)
        to_b[slot, plain, :] = second.astype(BF16)
    parts = [ref[...] for ref in scale_refs]
    if step == 3:
        scale = four(parts)
        put_scale(to_a.at[0], scale)
        put_scale(to_b.at[0], scale)
    elif step == 2:
        other = get_scale(sent_b.at[0])
        scale = get_scale(sent_a.at[0]) + other
        put_scale(to_a.at[0], other)
        put_scale(to_b.at[0], other)
    else:
        scale = (parts[0] + get_scale(sent_a.at[0])) + parts[1]
    if step > 1:
        for ref in (to_a, to_b):
            ref[1, 2 * ROWS :, :] = jnp.zeros((32, 2 * ROWS), BF16)
    scale_out[...] = scale


def last_hop_body(near, sent_a, sent_b, *refs):
    scale_refs, (ours, theirs, scale_out) = refs[:4], refs[4:]
    first = near[0] + sent_a[0].astype(F32) + sent_b[0].astype(F32)
    ours[...] = first.astype(BF16)
    second = near[1] + sent_a[1].astype(F32) + sent_b[1].astype(F32)
    theirs[...] = second.astype(BF16)
    scale_out[...] = four([ref[...] for ref in scale_refs])


def place(blocks, first, top, key_c, value_c, pos_c):
    start = jnp.int32(0)
    entries = []
    for phase in range(2):
        slot = first if phase == 0 else 1 - first
        rows = [positions(ref, slot) for ref in blocks]
        begins = [jnp.min(row) for row in rows]
        counts = [jnp.sum(jnp.where(row < FAR, 1.0, 0.0)).astype(jnp.int32) for row in rows]
        counts = [jnp.where(begin <= top, n, 0) for begin, n in zip(begins, counts)]
        spans = [(n + 15) >> 4 for n in counts]
        def put(number, at, slot=slot, rows=rows):
            ref = blocks[number]
            target = pl.ds(pl.multiple_of(at, 16), ROWS)
            pos_c[target, :] = jnp.broadcast_to(rows[number], (ROWS, ROWS)).T
            for g in range(KV_HEADS):
                lanes = slice(g * HEAD, (g + 1) * HEAD)
                key_c[g, target, :] = ref[slot, POS : POS + ROWS, lanes]
                value_c[g, target, :] = ref[slot, POS + ROWS : MESSAGE, lanes]

        if len(blocks) == 2:
            ahead = begins[0] < begins[1]
            starts = [
                start + jnp.where(ahead, 0, spans[1] * 16),
                start + jnp.where(ahead, spans[0] * 16, 0),
            ]

            @pl.when(ahead)
            def _():
                put(0, starts[0])
                put(1, starts[1])

            @pl.when(jnp.logical_not(ahead))
            def _():
                put(1, starts[1])
                put(0, starts[0])

        else:
            starts = []
            total = start
            for number, span in enumerate(spans):
                starts.append(total)
                put(number, total)
                total = total + span * 16
        entries.append((slot, starts, counts))
        start = start + sum(spans) * 16
    rest = pl.ds(pl.multiple_of(start, 16), TILE)
    pos_c[rest, :] = jnp.full((TILE, ROWS), 1e9, F32)
    for g in range(KV_HEADS):
        key_c[g, rest, :] = jnp.zeros((TILE, HEAD), BF16)
        value_c[g, rest, :] = jnp.zeros((TILE, HEAD), BF16)
    return start, entries


def stats_tile(rate_ref, work_ref, state, key_c, value_c, mask, at, slot, g):
    some = slice(g * WIDE, (g + 1) * WIDE)
    raw = product(key_c[g, pl.ds(at, TILE), :], work_ref[0, some, :], NT)
    dots = product(value_c[g, pl.ds(at, TILE), :], work_ref[1, some, :], NT)
    for head in range(GROUP):
        lanes = slice(head * ROWS, (head + 1) * ROWS)
        scores = jnp.where(mask, raw[:, lanes] * rate_ref[g, 0:1, lanes], LOW)
        held = [state[slot * KV_HEADS + g, n, :, lanes] for n in range(5)]
        top, total, weighted, shifted, both = held
        scores = scores.reshape(TILE // 8, 8, ROWS)
        new_top = jnp.maximum(top, jnp.max(scores, axis=0))
        above = scores - new_top[None]
        weights = jnp.exp2(above)
        weighted_dots = weights * dots[:, lanes].reshape(TILE // 8, 8, ROWS)
        step_down = top - new_top
        factor = jnp.exp2(step_down)
        held = [
            new_top,
            factor * total + jnp.sum(weights, axis=0),
            factor * weighted + jnp.sum(weighted_dots, axis=0),
            factor * (shifted + step_down * total) + jnp.sum(weights * above, axis=0),
            factor * (both + step_down * weighted) + jnp.sum(weighted_dots * above, axis=0),
        ]
        for n in range(5):
            state[slot * KV_HEADS + g, n, :, lanes] = held[n]


def stats_body(jobs, is_first, is_last, *refs):
    rate_ref, own_ref, kept_ref, got_ref = refs[:4]
    refs = refs[4:]
    work = []
    for count, slots in jobs:
        work.append((refs[:count], slots))
        refs = refs[count:]
    if not is_first:
        prior_ref, refs = refs[0], refs[1:]
    if is_last:
        final_ref, scale_ref, state, key_c, value_c, pos_c = refs
    else:
        state, token_ref, key_c, value_c, pos_c = refs
        token_ref[...] = jnp.zeros_like(token_ref)
    query_rows, tops, first = query_side(own_ref)
    if is_first:
        state[...] = jnp.zeros_like(state)
        state[:, 0] = jnp.full((2 * KV_HEADS, 8, WIDE), LOW, F32)
    else:
        state[...] = prior_ref[...]
    for blocks, slots in work:
        top = jnp.maximum(tops[0], tops[1]) if len(slots) == 2 else tops[slots[0]]
        length, _ = place(blocks, first, top, key_c, value_c, pos_c)

        def tile(step, _, slots=slots):
            at = pl.multiple_of(step * TILE, TILE)
            key_pos = pos_c[pl.ds(at, TILE), :]
            lowest = jnp.min(key_pos)
            for slot in slots:

                @pl.when(lowest <= tops[slot])
                def _(slot=slot):
                    mask = key_pos <= query_rows[slot]
                    for g in range(KV_HEADS):
                        stats_tile(
                            rate_ref, (kept_ref, got_ref)[slot], state, key_c, value_c, mask, at, slot, g
                        )

            return 0

        lax.fori_loop(0, (length + TILE - 1) // TILE, tile, 0)
    if not is_last:
        return
    lane = lax.broadcasted_iota(jnp.int32, (8, ROWS), 1)
    scale_row = jnp.zeros((8, ROWS), F32)
    for slot in range(2):
        live = query_rows[slot] >= 0.0
        for g in range(KV_HEADS):
            for head in range(GROUP):
                lanes = slice(head * ROWS, (head + 1) * ROWS)
                held = [state[slot * KV_HEADS + g, n, :, lanes] for n in range(5)]
                tops_in, total, weighted, shifted, both = held
                top = jnp.max(tops_in, axis=0, keepdims=True)
                step_down = tops_in - top
                factor = jnp.exp2(step_down)
                both = jnp.sum(factor * (both + step_down * weighted), axis=0, keepdims=True)
                shifted = jnp.sum(factor * (shifted + step_down * total), axis=0, keepdims=True)
                weighted = jnp.sum(factor * weighted, axis=0, keepdims=True)
                total = jnp.sum(factor * total, axis=0, keepdims=True)
                total = jnp.where(live, total, 1.0)
                mean = weighted / total
                spread = (both - mean * shifted) / total
                rate = rate_ref[g, 0:1, lanes] * math.sqrt(HEAD)
                spread = jnp.where(live, spread / rate, 0.0)
                final_ref[slot * KV_HEADS + g, 0:2, lanes] = jnp.concatenate(
                    [
                        jnp.where(live, top + jnp.log2(total), -LOW),
                        jnp.where(live, mean, 0.0),
                    ],
                    axis=0,
                )
                place_at = first * HEADS + g * GROUP + head
                scale_row = scale_row + jnp.where(
                    lane == place_at, jnp.sum(spread, axis=1, keepdims=True), 0.0
                )
    scale_ref[...] = scale_row


def grads_tile(
    rate_ref,
    work_ref,
    final_ref,
    key_c,
    value_c,
    key_sum,
    value_sum,
    query_sum,
    mask,
    at,
    slot,
    g,
):
    some = slice(g * WIDE, (g + 1) * WIDE)
    rows = pl.ds(at, TILE)
    keys = key_c[g, rows, :]
    values = value_c[g, rows, :]
    queries = work_ref[0, some, :]
    gradients = work_ref[1, some, :]
    raw = product(keys, queries, NT)
    dots = product(values, gradients, NT)
    probs, score_grads = [], []
    for head in range(GROUP):
        lanes = slice(head * ROWS, (head + 1) * ROWS)
        rate = rate_ref[g, 0:1, lanes]
        held = final_ref[slot * KV_HEADS + g, :, lanes]
        prob = jnp.where(mask, jnp.exp2(raw[:, lanes] * rate - held[0:1]), 0.0)
        grad = prob * (dots[:, lanes] - held[1:2])
        probs.append(prob.astype(BF16))
        score_grads.append((grad * (rate * (1.0 / LOG2E))).astype(BF16))
    prob_low = jnp.concatenate(probs, axis=1)
    score_low = jnp.concatenate(score_grads, axis=1)
    value_sum[g, rows, :] += product(prob_low, gradients, NN)
    key_sum[g, rows, :] += product(score_low, queries, NN)
    query_sum[slot * KV_HEADS + g] += product(keys, score_low, TN)


def grads_body(count, is_first, is_last, *refs):
    rate_ref, own_ref, kept_ref, got_ref, final_ref = refs[:5]
    blocks = refs[5 : 5 + count]
    refs = refs[5 + count :]
    if not is_first:
        prior_ref, refs = refs[0], refs[1:]
    outs, refs = refs[:count], refs[count:]
    if is_last:
        query_outs, refs = refs[:2], refs[2:]
    query_sum, key_c, value_c, pos_c, key_sum, value_sum = refs
    query_rows, tops, first = query_side(own_ref)
    length, entries = place(
        blocks, first, jnp.maximum(tops[0], tops[1]), key_c, value_c, pos_c
    )
    if is_first:
        query_sum[...] = jnp.zeros_like(query_sum)
    else:
        query_sum[...] = prior_ref[...]

    def tile(step, _):
        at = pl.multiple_of(step * TILE, TILE)
        key_pos = pos_c[pl.ds(at, TILE), :]
        lowest = jnp.min(key_pos)
        for g in range(KV_HEADS):
            key_sum[g, pl.ds(at, TILE), :] = jnp.zeros((TILE, HEAD), F32)
            value_sum[g, pl.ds(at, TILE), :] = jnp.zeros((TILE, HEAD), F32)
        for slot in range(2):

            @pl.when(lowest <= tops[slot])
            def _(slot=slot):
                mask = key_pos <= query_rows[slot]
                for g in range(KV_HEADS):
                    grads_tile(
                        rate_ref,
                        (kept_ref, got_ref)[slot],
                        final_ref,
                        key_c,
                        value_c,
                        key_sum,
                        value_sum,
                        query_sum,
                        mask,
                        at,
                        slot,
                        g,
                    )

        return 0

    lax.fori_loop(0, (length + TILE - 1) // TILE, tile, 0)
    row = lax.broadcasted_iota(jnp.int32, (ROWS, HEAD), 0)
    for slot, starts, counts in entries:
        for out, at, n in zip(outs, starts, counts):
            at = pl.multiple_of(at, 16)
            for g in range(KV_HEADS):
                lanes = slice(g * HEAD, (g + 1) * HEAD)
                for number, total in enumerate((key_sum, value_sum)):
                    out[slot, number * ROWS : (number + 1) * ROWS, lanes] = jnp.where(
                        row < n, total[g, pl.ds(at, ROWS), :], 0.0
                    )
    if is_last:
        for slot in range(2):
            for g in range(KV_HEADS):
                for head in range(GROUP):
                    lanes = slice(head * ROWS, (head + 1) * ROWS)
                    rows = slice((g * GROUP + head) * ROWS, (g * GROUP + head + 1) * ROWS)
                    query_outs[slot][rows, :] = query_sum[slot * KV_HEADS + g, :, lanes].T.astype(
                        BF16
                    )


def compact_scratch(count):
    size = 2 * count * ROWS + TILE
    return [
        pltpu.VMEM((KV_HEADS, size, HEAD), BF16),
        pltpu.VMEM((KV_HEADS, size, HEAD), BF16),
        pltpu.VMEM((size, ROWS), F32),
    ]


STATE = jax.ShapeDtypeStruct((2 * KV_HEADS, 5, 8, WIDE), F32)
SMALL = jax.ShapeDtypeStruct((8, ROWS), F32)
FINAL = jax.ShapeDtypeStruct((2 * KV_HEADS, 8, WIDE), F32)


def stats(rate, own, kept, got, jobs, prior=None, is_last=False):
    if is_last:
        outs = [FINAL, jax.ShapeDtypeStruct((8, ROWS), F32)]
        scratch = [pltpu.VMEM(STATE.shape, F32)]
    else:
        outs, scratch = [STATE, SMALL], []
    blocks = [block for some, _ in jobs for block in some]
    operands = [rate, own, kept, got, *blocks] + ([] if prior is None else [prior])
    sizes = [(len(some), slots) for some, slots in jobs]
    return call(
        functools.partial(stats_body, sizes, prior is None, is_last),
        outs,
        scratch + compact_scratch(max(count for count, _ in sizes)),
        sum(count * len(slots) for count, slots in sizes) * ROWS * 2 * HEADS * ROWS * HEAD * 4,
        4 << 20,
        [pl.BlockSpec(memory_space=pltpu.VMEM)] * len(operands),
    )(*operands)


def grads(rate, own, kept, got, final, blocks, prior=None, is_last=False):
    count = len(blocks)
    outs = [jax.ShapeDtypeStruct((2, 2 * ROWS, KV_HEADS * HEAD), F32)] * count
    sums = jax.ShapeDtypeStruct((2 * KV_HEADS, HEAD, WIDE), F32)
    operands = [rate, own, kept, got, final, *blocks]
    operands = operands + ([] if prior is None else [prior])
    if is_last:
        outs = outs + [jax.ShapeDtypeStruct((HEADS * ROWS, HEAD), BF16)] * 2
        scratch = [pltpu.VMEM(sums.shape, F32)]
    else:
        outs, scratch = outs + [sums], []
    size = 2 * count * ROWS + TILE
    scratch = (
        scratch
        + compact_scratch(count)
        + [pltpu.VMEM((KV_HEADS, size, HEAD), F32), pltpu.VMEM((KV_HEADS, size, HEAD), F32)]
    )
    return call(
        functools.partial(grads_body, count, prior is None, is_last),
        outs,
        scratch,
        count * 2 * ROWS * 2 * HEADS * ROWS * 2 * HEAD * 5,
        6 << 20,
        [pl.BlockSpec(memory_space=pltpu.VMEM)] * len(operands),
    )(*operands)


def local(queries, keys, values, out_grad, routes, per_head_scale):
    me = lax.axis_index("ctx")
    size = lax.axis_size("ctx")
    ring = size // 2
    x = (me // ring).astype(jnp.int32)
    x_ref = x.reshape(1)
    across = [(i, (i + ring) % size) for i in range(size)]

    def neighbour(i, up):
        base, z = i // ring * ring, i % ring
        return base + (z + (1 if up == (z % 2 == 0) else -1)) % ring

    even = [(i, neighbour(i, True)) for i in range(size)]
    odd = [(i, neighbour(i, False)) for i in range(size)]

    def swap(array, pairs, axis="ctx"):
        return lax.ppermute(array, axis, pairs)

    smem = pl.BlockSpec(memory_space=pltpu.SMEM)
    vmem = pl.BlockSpec(memory_space=pltpu.VMEM)
    anywhere = pl.BlockSpec(memory_space=pl.ANY)
    in_hbm = pl.BlockSpec(memory_space=pltpu.HBM)
    width = KV_HEADS * HEAD
    message = jax.ShapeDtypeStruct((MESSAGE, width), BF16)
    keys_kept, keys_sent = call(
        pack_keys_body,
        [message, message],
        [
            pltpu.VMEM((ROWS, 2 * width), BF16),
            pltpu.VMEM((ROWS, 2 * width), BF16),
            pltpu.VMEM((1, ROWS), jnp.int32),
            pltpu.SemaphoreType.DMA((3,)),
        ],
        1024,
        1 << 20,
        [smem, in_hbm, in_hbm, in_hbm],
    )(x_ref, keys[0], values[0], routes)
    keys_got = swap(keys_sent, across)
    work = jax.ShapeDtypeStruct((2, HEADS * ROWS, HEAD), BF16)
    kept, sent = call(
        pack_queries_body,
        [work, work],
        [
            pltpu.VMEM((ROWS, 2 * HEADS * HEAD), BF16),
            pltpu.VMEM((ROWS, 2 * HEADS * HEAD), BF16),
            pltpu.SemaphoreType.DMA((2,)),
        ],
        1024,
        4 << 20,
        [smem, anywhere, in_hbm, in_hbm],
    )(x_ref, keys_sent, queries[0], out_grad[0])
    got = swap(sent, across)
    own = call(
        join_body,
        jax.ShapeDtypeStruct((2, MESSAGE, width), BF16),
        [],
        1024,
        1 << 20,
        [anywhere, vmem, vmem],
    )(kept, keys_kept, keys_got)

    half_scale = lax.dynamic_slice_in_dim(per_head_scale, x * HEADS, HEADS)
    rate = jnp.repeat(half_scale * (LOG2E / math.sqrt(HEAD)), ROWS).reshape(KV_HEADS, 1, WIDE)
    rate = jnp.broadcast_to(rate, (KV_HEADS, 8, WIDE))

    def gate(blocks, after):
        def body(*refs):
            for source, target in zip(refs, refs[len(blocks) + 1 :]):
                target[...] = source[...]

        return call(
            body,
            [jax.ShapeDtypeStruct(block.shape, block.dtype) for block in blocks],
            [],
            1024,
            1 << 20,
            [vmem] * (len(blocks) + 1),
        )(*blocks, after)

    a, b = [own], [own]
    a.append(swap(own, even))
    b.append(swap(own, odd))
    state, token = stats(rate, own, kept, kept, [([own], (0,))])
    a[1], b[1] = gate([a[1], b[1]], token)
    a.append(swap(b[1], even))
    b.append(swap(a[1], odd))
    state, token = stats(rate, own, kept, kept, [([a[1], b[1]], (0,))], state)
    a[2], b[2] = gate([a[2], b[2]], token)
    a.append(swap(b[2], even))
    b.append(swap(a[2], odd))
    state, token = stats(rate, own, kept, kept, [([a[2], b[2]], (0,))], state)
    a[3], b[3] = gate([a[3], b[3]], token)
    a.append(swap(b[3], even))
    jobs = [([own, a[1], b[1], a[2], b[2]], (1,)), ([a[3], b[3]], (0, 1))]
    state, token = stats(rate, own, kept, got, jobs, state)
    final, scale = stats(rate, own, kept, got, [([a[4]], (0, 1))], state, is_last=True)

    total_devices = lax.axis_size("dp") * size

    def exchange(array, masks):
        pairs = [[(i, i ^ mask) for i in range(total_devices)] for mask in masks]
        return [array] + [swap(array, pair, ("dp", "ctx")) for pair in pairs]

    def hop(step, parts, arrived, scales=()):
        out = jax.ShapeDtypeStruct((2, 2 * ROWS + (32 if step > 1 else 0), width), BF16)
        return call(
            functools.partial(hop_body, step, len(scales)),
            [out, out, SMALL],
            [],
            1024,
            2 << 20,
            [vmem] * (2 + len(arrived) + len(scales)),
        )(*parts, *arrived, *scales)

    scales = exchange(scale, (4, 8, 12))
    far, sums = grads(rate, own, kept, got, final, [a[4]])
    from_even = swap(far.astype(BF16), even)
    part_a, part_b, sums = grads(rate, own, kept, got, final, [a[3], b[3]], sums)
    to_a, to_b, scale = hop(3, (part_a, part_b), (from_even,), scales)
    sent_a, sent_b = swap(to_a, even), swap(to_b, odd)
    part_a, part_b, near, sums = grads(rate, own, kept, got, final, [a[2], b[2], own], sums)
    to_a, to_b, beside = hop(2, (part_a, part_b), (sent_a, sent_b))
    sent_a, sent_b = swap(to_a, even), swap(to_b, odd)
    part_a, part_b, query_kept, query_sent = grads(
        rate, own, kept, got, final, [a[1], b[1]], sums, is_last=True
    )
    query_got = swap(query_sent, across)
    to_a, to_b, scale = hop(1, (part_a, part_b), (sent_a, sent_b), [scale, beside])
    sent_a, sent_b = swap(to_a, even), swap(to_b, odd)
    scales = exchange(scale, (64, 128, 192))
    ours, theirs, scale = call(
        last_hop_body,
        [jax.ShapeDtypeStruct((2 * ROWS, width), BF16)] * 2 + [SMALL],
        [],
        1024,
        2 << 20,
        [vmem] * 7,
    )(near, sent_a, sent_b, *scales)
    other = swap(theirs, across)
    scales = exchange(scale, (16, 32, 48))
    query_out, key_out, value_out, scale_out = call(
        finish_body,
        [
            jax.ShapeDtypeStruct((ROWS, 2 * HEADS * HEAD), BF16),
            jax.ShapeDtypeStruct((ROWS, 2 * width), BF16),
            jax.ShapeDtypeStruct((ROWS, 2 * width), BF16),
            jax.ShapeDtypeStruct((1, 2 * HEADS), F32),
        ],
        [],
        1024,
        2 << 20,
        [smem] + [vmem] * 8,
    )(x_ref, query_kept, query_got, ours, other, *scales)
    return query_out[None], key_out[None], value_out[None], scale_out.reshape(2 * HEADS)


def solution(mesh):
    in_specs = (
        P("dp", "ctx", None),
        P("dp", "ctx", None),
        P("dp", "ctx", None),
        P("dp", "ctx", None),
        P("dp", "ctx"),
        P(),
    )
    out_specs = (P("dp", "ctx", None), P("dp", "ctx", None), P("dp", "ctx", None), P())
    return jax.shard_map(local, mesh=mesh, in_specs=in_specs, out_specs=out_specs, check_vma=False)
```

```python
import functools
import math

import jax
import jax.numpy as jnp
from jax import lax
from jax.experimental import pallas as pl
from jax.experimental.pallas import tpu as pltpu
from jax.sharding import PartitionSpec as P

F32 = jnp.float32
BF16 = jnp.bfloat16
HEAD = 128
ROWS = 128
KV_HEADS = 2
GROUP = 7
HEADS = KV_HEADS * GROUP
WIDE = GROUP * ROWS
POS = 16
MESSAGE = POS + 2 * ROWS
TILE = 128
FAR = 32768.0
LOW = -1e30
LOG2E = 1.4426950408889634
NT = (((1,), (1,)), ((), ()))
NN = (((1,), (0,)), ((), ()))
TN = (((0,), (0,)), ((), ()))


def product(a, b, dims):
    return lax.dot_general(a, b, dims, preferred_element_type=F32)


def call(body, outs, scratch, flops, moved, operands, limit=10, aliases=None):
    return pl.pallas_call(
        body,
        out_shape=outs,
        in_specs=operands,
        scratch_shapes=scratch,
        input_output_aliases=aliases or {},
        cost_estimate=pl.CostEstimate(
            flops=flops, bytes_accessed=moved, transcendentals=flops // 1024
        ),
        compiler_params=pltpu.CompilerParams(vmem_limit_bytes=limit * 1024 * 1024),
    )


def fetch(sources, targets, sem):
    copies = [
        pltpu.make_async_copy(source, target, sem.at[n])
        for n, (source, target) in enumerate(zip(sources, targets))
    ]
    for copy in copies:
        copy.start()
    for copy in copies:
        copy.wait()


def pack_keys_body(x_ref, key_in, value_in, pos_in, keep_ref, send_ref, key_ref, value_ref, pos_ref, sem):
    x = x_ref[0]
    fetch((key_in, value_in, pos_in), (key_ref, value_ref, pos_ref), sem)
    pos = pos_ref[...]
    dead = pos < 0
    high = jnp.where(dead, 256, pos >> 7)
    low = jnp.where(dead, 0, pos & 127)
    row = jnp.concatenate([high, low], axis=1).astype(F32)
    rows = jnp.broadcast_to(row, (POS, 2 * ROWS)).astype(BF16)
    for ref, half in ((keep_ref, x), (send_ref, 1 - x)):
        at = pl.multiple_of(half * KV_HEADS * HEAD, KV_HEADS * HEAD)
        ref[0:POS, :] = rows
        ref[POS : POS + ROWS, :] = key_ref[:, pl.ds(at, KV_HEADS * HEAD)]
        ref[POS + ROWS : MESSAGE, :] = value_ref[:, pl.ds(at, KV_HEADS * HEAD)]


def pack_queries_body(x_ref, after_ref, query_in, grad_in, keep_ref, send_ref, query_ref, grad_ref, sem):
    x = x_ref[0]
    fetch((query_in, grad_in), (query_ref, grad_ref), sem)
    for ref, half in ((send_ref, 1 - x), (keep_ref, x)):
        for number, source in enumerate((query_ref, grad_ref)):
            for head in range(HEADS):
                at = pl.multiple_of(half * HEADS * HEAD + head * HEAD, HEAD)
                ref[number, head * ROWS : (head + 1) * ROWS, :] = source[:, pl.ds(at, HEAD)]


def join_body(after_ref, keep_ref, got_ref, out_ref):
    out_ref[0] = keep_ref[...]
    out_ref[1] = got_ref[...]


def finish_body(
    x_ref,
    keep_ref,
    got_ref,
    own_ref,
    other_ref,
    *refs,
):
    scale_refs, (query_out, key_out, value_out, scale_out) = refs[:4], refs[4:]
    x = x_ref[0]
    scale = four([ref[...] for ref in scale_refs])
    scale_out[...] = scale[0:1, : 2 * HEADS]
    for ref, half in ((own_ref, x), (other_ref, 1 - x)):
        at = pl.multiple_of(half * KV_HEADS * HEAD, KV_HEADS * HEAD)
        key_out[:, pl.ds(at, KV_HEADS * HEAD)] = ref[:ROWS, :]
        value_out[:, pl.ds(at, KV_HEADS * HEAD)] = ref[ROWS : 2 * ROWS, :]
    for ref, half in ((keep_ref, x), (got_ref, 1 - x)):
        for head in range(HEADS):
            at = pl.multiple_of(half * HEADS * HEAD + head * HEAD, HEAD)
            query_out[:, pl.ds(at, HEAD)] = ref[head * ROWS : (head + 1) * ROWS, :]


def positions(ref, slot):
    row = ref[slot, 0:POS, :].astype(F32)[0:1, :]
    return row[:, :ROWS] * 128.0 + row[:, ROWS:]


def query_side(own_ref):
    rows = [positions(own_ref, slot) for slot in range(2)]
    rows = [jnp.where(row >= FAR, -1.0, row) for row in rows]
    tops = [jnp.max(row) for row in rows]
    first = jnp.where(tops[0] < tops[1], 0, 1)
    return rows, tops, first


def four(parts):
    return (parts[0] + parts[1]) + (parts[2] + parts[3])


def code(value):
    high = value.astype(BF16)
    value = value - high.astype(F32)
    middle = value.astype(BF16)
    return [high, middle, (value - middle.astype(F32)).astype(BF16)]


def put_scale(ref, scale):
    for number, part in enumerate(code(scale)):
        lanes = slice(0, ROWS) if number < 2 else slice(ROWS, 2 * ROWS)
        rows = jnp.concatenate([part] * 2, axis=0)
        at = 2 * ROWS + (number % 2) * 16
        ref[at : at + 16, lanes] = rows
    ref[2 * ROWS + 16 : 2 * ROWS + 32, ROWS : 2 * ROWS] = jnp.zeros((16, ROWS), BF16)


def get_scale(ref):
    at = 2 * ROWS
    high = ref[at : at + 16, :ROWS].astype(F32)
    middle = ref[at + 16 : at + 32, :ROWS].astype(F32)
    low = ref[at : at + 16, ROWS:].astype(F32)
    return ((high + middle) + low)[0:8]


def hop_body(step, count, *refs):
    part_a, part_b, sent_a = refs[:3]
    refs = refs[3:]
    if step < 3:
        sent_b, refs = refs[0], refs[1:]
    scale_refs, (to_a, to_b, scale_out) = refs[:count], refs[count:]
    plain = slice(0, 2 * ROWS)
    for slot in range(2):
        first = part_a[slot]
        if step < 3:
            first = first + sent_b[slot, plain, :].astype(F32)
        to_a[slot, plain, :] = first.astype(BF16)
        second = part_b[slot] + sent_a[slot, plain, :].astype(F32)
        to_b[slot, plain, :] = second.astype(BF16)
    parts = [ref[...] for ref in scale_refs]
    if step == 3:
        scale = parts[0] + parts[1]
        put_scale(to_a.at[0], scale)
        put_scale(to_b.at[0], scale)
    elif step == 2:
        other = get_scale(sent_b.at[0])
        scale = get_scale(sent_a.at[0]) + other
        put_scale(to_a.at[0], other)
        put_scale(to_b.at[0], other)
    else:
        scale = (parts[0] + get_scale(sent_a.at[0])) + parts[1]
    if step > 1:
        for ref in (to_a, to_b):
            ref[1, 2 * ROWS :, :] = jnp.zeros((32, 2 * ROWS), BF16)
    scale_out[...] = scale


def last_hop_body(near, sent_a, sent_b, *refs):
    scale_refs, (ours, theirs, scale_out) = refs[:4], refs[4:]
    first = near[0] + sent_a[0].astype(F32) + sent_b[0].astype(F32)
    ours[...] = first.astype(BF16)
    second = near[1] + sent_a[1].astype(F32) + sent_b[1].astype(F32)
    theirs[...] = second.astype(BF16)
    scale_out[...] = four([ref[...] for ref in scale_refs])


def place(blocks, first, top, key_c, value_c, pos_c, span=TILE):
    start = jnp.int32(0)
    entries = []
    for phase in range(2):
        slot = first if phase == 0 else 1 - first
        rows = [positions(ref, slot) for ref in blocks]
        begins = [jnp.min(row) for row in rows]
        counts = [jnp.sum(jnp.where(row < FAR, 1.0, 0.0)).astype(jnp.int32) for row in rows]
        counts = [jnp.where(begin <= top, n, 0) for begin, n in zip(begins, counts)]
        chunks = [(n + 15) >> 4 for n in counts]
        def put(number, at, slot=slot, rows=rows):
            ref = blocks[number]
            target = pl.ds(pl.multiple_of(at, 16), ROWS)
            pos_c[target, :] = jnp.broadcast_to(rows[number], (ROWS, ROWS)).T
            for g in range(KV_HEADS):
                lanes = slice(g * HEAD, (g + 1) * HEAD)
                key_c[g, target, :] = ref[slot, POS : POS + ROWS, lanes]
                value_c[g, target, :] = ref[slot, POS + ROWS : MESSAGE, lanes]

        if len(blocks) == 2:
            ahead = begins[0] < begins[1]
            starts = [
                start + jnp.where(ahead, 0, chunks[1] * 16),
                start + jnp.where(ahead, chunks[0] * 16, 0),
            ]

            @pl.when(ahead)
            def _():
                put(0, starts[0])
                put(1, starts[1])

            @pl.when(jnp.logical_not(ahead))
            def _():
                put(1, starts[1])
                put(0, starts[0])

        else:
            starts = []
            total = start
            for number, chunk in enumerate(chunks):
                starts.append(total)
                put(number, total)
                total = total + chunk * 16
        entries.append((slot, starts, counts))
        start = start + sum(chunks) * 16
    rest = pl.ds(pl.multiple_of(start, 16), span)
    pos_c[rest, :] = jnp.full((span, ROWS), 1e9, F32)
    for g in range(KV_HEADS):
        key_c[g, rest, :] = jnp.zeros((span, HEAD), BF16)
        value_c[g, rest, :] = jnp.zeros((span, HEAD), BF16)
    return start, entries


def tile_of(blocks):
    return 2 * TILE if len(blocks) > 2 else TILE


def stats_tile(rate_ref, work_ref, state, key_c, value_c, mask, rows, slot, g):
    some = slice(g * WIDE, (g + 1) * WIDE)
    raw = product(key_c[g, rows, :], work_ref[0, some, :], NT)
    dots = product(value_c[g, rows, :], work_ref[1, some, :], NT)
    for head in range(GROUP):
        lanes = slice(head * ROWS, (head + 1) * ROWS)
        scores = jnp.where(mask, raw[:, lanes] * rate_ref[g, 0:1, lanes], LOW)
        held = [state[slot * KV_HEADS + g, n, :, lanes] for n in range(5)]
        top, total, weighted, shifted, both = held
        scores = scores.reshape(mask.shape[0] // 8, 8, ROWS)
        new_top = jnp.maximum(top, jnp.max(scores, axis=0))
        above = scores - new_top[None]
        weights = jnp.exp2(above)
        weighted_dots = weights * dots[:, lanes].reshape(mask.shape[0] // 8, 8, ROWS)
        step_down = top - new_top
        factor = jnp.exp2(step_down)
        held = [
            new_top,
            factor * total + jnp.sum(weights, axis=0),
            factor * weighted + jnp.sum(weighted_dots, axis=0),
            factor * (shifted + step_down * total) + jnp.sum(weights * above, axis=0),
            factor * (both + step_down * weighted) + jnp.sum(weighted_dots * above, axis=0),
        ]
        for n in range(5):
            state[slot * KV_HEADS + g, n, :, lanes] = held[n]


def stats_body(jobs, is_first, is_last, *refs):
    rate_ref, own_ref, kept_ref, got_ref = refs[:4]
    refs = refs[4:]
    work = []
    for count, slots in jobs:
        work.append((refs[:count], slots))
        refs = refs[count:]
    if not is_first:
        prior_ref, refs = refs[0], refs[1:]
    if is_last:
        final_ref, scale_ref, state, key_c, value_c, pos_c = refs
    else:
        state, token_ref, key_c, value_c, pos_c = refs
        token_ref[...] = jnp.zeros_like(token_ref)
    query_rows, tops, first = query_side(own_ref)
    if is_first:
        state[...] = jnp.zeros_like(state)
        state[:, 0] = jnp.full((2 * KV_HEADS, 8, WIDE), LOW, F32)
    else:
        state[...] = prior_ref[...]
    for blocks, slots in work:
        span = tile_of(blocks)
        top = jnp.maximum(tops[0], tops[1]) if len(slots) == 2 else tops[slots[0]]
        length, _ = place(blocks, first, top, key_c, value_c, pos_c, span)

        def tile(step, _, slots=slots, span=span):
            at = pl.multiple_of(step * span, span)
            key_pos = pos_c[pl.ds(at, span), :]
            lowest = jnp.min(key_pos)
            for slot in slots:

                @pl.when(lowest <= tops[slot])
                def _(slot=slot):
                    mask = key_pos <= query_rows[slot]
                    for g in range(KV_HEADS):
                        stats_tile(
                            rate_ref,
                            (kept_ref, got_ref)[slot],
                            state,
                            key_c,
                            value_c,
                            mask,
                            pl.ds(at, span),
                            slot,
                            g,
                        )

            return 0

        lax.fori_loop(0, (length + span - 1) // span, tile, 0)
    if not is_last:
        return
    lane = lax.broadcasted_iota(jnp.int32, (8, ROWS), 1)
    scale_row = jnp.zeros((8, ROWS), F32)
    for slot in range(2):
        live = query_rows[slot] >= 0.0
        for g in range(KV_HEADS):
            for head in range(GROUP):
                lanes = slice(head * ROWS, (head + 1) * ROWS)
                held = [state[slot * KV_HEADS + g, n, :, lanes] for n in range(5)]
                tops_in, total, weighted, shifted, both = held
                top = jnp.max(tops_in, axis=0, keepdims=True)
                step_down = tops_in - top
                factor = jnp.exp2(step_down)
                both = jnp.sum(factor * (both + step_down * weighted), axis=0, keepdims=True)
                shifted = jnp.sum(factor * (shifted + step_down * total), axis=0, keepdims=True)
                weighted = jnp.sum(factor * weighted, axis=0, keepdims=True)
                total = jnp.sum(factor * total, axis=0, keepdims=True)
                total = jnp.where(live, total, 1.0)
                mean = weighted / total
                spread = (both - mean * shifted) / total
                rate = rate_ref[g, 0:1, lanes] * math.sqrt(HEAD)
                spread = jnp.where(live, spread / rate, 0.0)
                final_ref[slot * KV_HEADS + g, 0:2, lanes] = jnp.concatenate(
                    [
                        jnp.where(live, top + jnp.log2(total), -LOW),
                        jnp.where(live, mean, 0.0),
                    ],
                    axis=0,
                )
                place_at = first * HEADS + g * GROUP + head
                scale_row = scale_row + jnp.where(
                    lane == place_at, jnp.sum(spread, axis=1, keepdims=True), 0.0
                )
    scale_ref[...] = scale_row


def grads_tile(
    rate_ref,
    work_ref,
    final_ref,
    key_c,
    value_c,
    key_sum,
    value_sum,
    query_sum,
    mask,
    at,
    slot,
    g,
):
    some = slice(g * WIDE, (g + 1) * WIDE)
    rows = pl.ds(at, TILE)
    keys = key_c[g, rows, :]
    values = value_c[g, rows, :]
    queries = work_ref[0, some, :]
    gradients = work_ref[1, some, :]
    raw = product(keys, queries, NT)
    dots = product(values, gradients, NT)
    probs, score_grads = [], []
    for head in range(GROUP):
        lanes = slice(head * ROWS, (head + 1) * ROWS)
        rate = rate_ref[g, 0:1, lanes]
        held = final_ref[slot * KV_HEADS + g, :, lanes]
        prob = jnp.where(mask, jnp.exp2(raw[:, lanes] * rate - held[0:1]), 0.0)
        grad = prob * (dots[:, lanes] - held[1:2])
        probs.append(prob.astype(BF16))
        score_grads.append((grad * (rate * (1.0 / LOG2E))).astype(BF16))
    prob_low = jnp.concatenate(probs, axis=1)
    score_low = jnp.concatenate(score_grads, axis=1)
    value_sum[g, rows, :] += product(prob_low, gradients, NN)
    key_sum[g, rows, :] += product(score_low, queries, NN)
    query_sum[slot * KV_HEADS + g] += product(keys, score_low, TN)


def grads_body(count, is_first, is_last, *refs):
    rate_ref, own_ref, kept_ref, got_ref, final_ref = refs[:5]
    blocks = refs[5 : 5 + count]
    refs = refs[5 + count :]
    if not is_first:
        prior_ref, refs = refs[0], refs[1:]
    outs, refs = refs[:count], refs[count:]
    if is_last:
        query_outs, refs = refs[:2], refs[2:]
    query_sum, key_c, value_c, pos_c, key_sum, value_sum = refs
    query_rows, tops, first = query_side(own_ref)
    length, entries = place(
        blocks, first, jnp.maximum(tops[0], tops[1]), key_c, value_c, pos_c
    )
    if is_first:
        query_sum[...] = jnp.zeros_like(query_sum)
    elif is_last:
        query_sum[...] = prior_ref[...]

    def tile(step, _):
        at = pl.multiple_of(step * TILE, TILE)
        key_pos = pos_c[pl.ds(at, TILE), :]
        lowest = jnp.min(key_pos)
        for g in range(KV_HEADS):
            key_sum[g, pl.ds(at, TILE), :] = jnp.zeros((TILE, HEAD), F32)
            value_sum[g, pl.ds(at, TILE), :] = jnp.zeros((TILE, HEAD), F32)
        for slot in range(2):

            @pl.when(lowest <= tops[slot])
            def _(slot=slot):
                mask = key_pos <= query_rows[slot]
                for g in range(KV_HEADS):
                    grads_tile(
                        rate_ref,
                        (kept_ref, got_ref)[slot],
                        final_ref,
                        key_c,
                        value_c,
                        key_sum,
                        value_sum,
                        query_sum,
                        mask,
                        at,
                        slot,
                        g,
                    )

        return 0

    lax.fori_loop(0, (length + TILE - 1) // TILE, tile, 0)
    row = lax.broadcasted_iota(jnp.int32, (ROWS, HEAD), 0)
    for slot, starts, counts in entries:
        for out, at, n in zip(outs, starts, counts):
            at = pl.multiple_of(at, 16)
            for g in range(KV_HEADS):
                lanes = slice(g * HEAD, (g + 1) * HEAD)
                for number, total in enumerate((key_sum, value_sum)):
                    out[slot, number * ROWS : (number + 1) * ROWS, lanes] = jnp.where(
                        row < n, total[g, pl.ds(at, ROWS), :], 0.0
                    )
    if is_last:
        for slot in range(2):
            for g in range(KV_HEADS):
                for head in range(GROUP):
                    lanes = slice(head * ROWS, (head + 1) * ROWS)
                    rows = slice((g * GROUP + head) * ROWS, (g * GROUP + head + 1) * ROWS)
                    query_outs[slot][rows, :] = query_sum[slot * KV_HEADS + g, :, lanes].T.astype(
                        BF16
                    )


def compact_scratch(count):
    size = 2 * count * ROWS + 2 * TILE
    return [
        pltpu.VMEM((KV_HEADS, size, HEAD), BF16),
        pltpu.VMEM((KV_HEADS, size, HEAD), BF16),
        pltpu.VMEM((size, ROWS), F32),
    ]


STATE = jax.ShapeDtypeStruct((2 * KV_HEADS, 5, 8, WIDE), F32)
SMALL = jax.ShapeDtypeStruct((8, ROWS), F32)
FINAL = jax.ShapeDtypeStruct((2 * KV_HEADS, 8, WIDE), F32)


def stats(rate, own, kept, got, jobs, prior=None, is_last=False):
    if is_last:
        outs = [FINAL, jax.ShapeDtypeStruct((8, ROWS), F32)]
        scratch = [pltpu.VMEM(STATE.shape, F32)]
    else:
        outs, scratch = [STATE, SMALL], []
    blocks = [block for some, _ in jobs for block in some]
    operands = [rate, own, kept, got, *blocks] + ([] if prior is None else [prior])
    sizes = [(len(some), slots) for some, slots in jobs]
    return call(
        functools.partial(stats_body, sizes, prior is None, is_last),
        outs,
        scratch + compact_scratch(max(count for count, _ in sizes)),
        sum(count * len(slots) for count, slots in sizes) * ROWS * 2 * HEADS * ROWS * HEAD * 4,
        4 << 20,
        [pl.BlockSpec(memory_space=pltpu.VMEM)] * len(operands),
    )(*operands)


def grads(rate, own, kept, got, final, blocks, prior=None, is_last=False):
    count = len(blocks)
    outs = [jax.ShapeDtypeStruct((2, 2 * ROWS, KV_HEADS * HEAD), F32)] * count
    sums = jax.ShapeDtypeStruct((2 * KV_HEADS, HEAD, WIDE), F32)
    operands = [rate, own, kept, got, final, *blocks]
    operands = operands + ([] if prior is None else [prior])
    if is_last:
        outs = outs + [jax.ShapeDtypeStruct((HEADS * ROWS, HEAD), BF16)] * 2
        scratch = [pltpu.VMEM(sums.shape, F32)]
    else:
        outs, scratch = outs + [sums], []
    aliases = {} if prior is None or is_last else {len(operands) - 1: len(outs) - 1}
    size = 2 * count * ROWS + TILE
    scratch = (
        scratch
        + compact_scratch(count)
        + [pltpu.VMEM((KV_HEADS, size, HEAD), F32), pltpu.VMEM((KV_HEADS, size, HEAD), F32)]
    )
    return call(
        functools.partial(grads_body, count, prior is None, is_last),
        outs,
        scratch,
        count * 2 * ROWS * 2 * HEADS * ROWS * 2 * HEAD * 5,
        6 << 20,
        [pl.BlockSpec(memory_space=pltpu.VMEM)] * len(operands),
        aliases=aliases,
    )(*operands)


def local(queries, keys, values, out_grad, routes, per_head_scale):
    me = lax.axis_index("ctx")
    size = lax.axis_size("ctx")
    ring = size // 2
    x = (me // ring).astype(jnp.int32)
    x_ref = x.reshape(1)
    across = [(i, (i + ring) % size) for i in range(size)]

    def neighbour(i, up):
        base, z = i // ring * ring, i % ring
        return base + (z + (1 if up == (z % 2 == 0) else -1)) % ring

    even = [(i, neighbour(i, True)) for i in range(size)]
    odd = [(i, neighbour(i, False)) for i in range(size)]

    def swap(array, pairs, axis="ctx"):
        return lax.ppermute(array, axis, pairs)

    smem = pl.BlockSpec(memory_space=pltpu.SMEM)
    vmem = pl.BlockSpec(memory_space=pltpu.VMEM)
    anywhere = pl.BlockSpec(memory_space=pl.ANY)
    in_hbm = pl.BlockSpec(memory_space=pltpu.HBM)
    width = KV_HEADS * HEAD
    message = jax.ShapeDtypeStruct((MESSAGE, width), BF16)
    keys_kept, keys_sent = call(
        pack_keys_body,
        [message, message],
        [
            pltpu.VMEM((ROWS, 2 * width), BF16),
            pltpu.VMEM((ROWS, 2 * width), BF16),
            pltpu.VMEM((1, ROWS), jnp.int32),
            pltpu.SemaphoreType.DMA((3,)),
        ],
        1024,
        1 << 20,
        [smem, in_hbm, in_hbm, in_hbm],
        60,
    )(x_ref, keys[0], values[0], routes)
    keys_got = swap(keys_sent, across)
    work = jax.ShapeDtypeStruct((2, HEADS * ROWS, HEAD), BF16)
    kept, sent = call(
        pack_queries_body,
        [work, work],
        [
            pltpu.VMEM((ROWS, 2 * HEADS * HEAD), BF16),
            pltpu.VMEM((ROWS, 2 * HEADS * HEAD), BF16),
            pltpu.SemaphoreType.DMA((2,)),
        ],
        1024,
        4 << 20,
        [smem, anywhere, in_hbm, in_hbm],
        60,
    )(x_ref, keys_sent, queries[0], out_grad[0])
    got = swap(sent, across)
    own = call(
        join_body,
        jax.ShapeDtypeStruct((2, MESSAGE, width), BF16),
        [],
        1024,
        1 << 20,
        [anywhere, vmem, vmem],
    )(sent, keys_kept, keys_got)

    half_scale = lax.dynamic_slice_in_dim(per_head_scale, x * HEADS, HEADS)
    rate = jnp.repeat(half_scale * (LOG2E / math.sqrt(HEAD)), ROWS).reshape(KV_HEADS, 1, WIDE)
    rate = jnp.broadcast_to(rate, (KV_HEADS, 8, WIDE))

    def gate(blocks, after):
        def body(*refs):
            for source, target in zip(refs, refs[len(blocks) + 1 :]):
                target[...] = source[...]

        return call(
            body,
            [jax.ShapeDtypeStruct(block.shape, block.dtype) for block in blocks],
            [],
            1024,
            1 << 20,
            [vmem] * (len(blocks) + 1),
        )(*blocks, after)

    a, b = [own], [own]
    a.append(swap(own, even))
    b.append(swap(own, odd))
    state, token = stats(rate, own, kept, kept, [([own], (0,))])
    a[1], b[1] = gate([a[1], b[1]], token)
    a.append(swap(b[1], even))
    b.append(swap(a[1], odd))
    state, token = stats(rate, own, kept, kept, [([a[1], b[1]], (0,))], state)
    a[2], b[2] = gate([a[2], b[2]], token)
    a.append(swap(b[2], even))
    b.append(swap(a[2], odd))
    state, token = stats(rate, own, kept, kept, [([a[2], b[2]], (0,))], state)
    a[3], b[3] = gate([a[3], b[3]], token)
    a.append(swap(b[3], even))
    jobs = [([own, a[1], b[1], a[2], b[2]], (1,)), ([a[3], b[3]], (0, 1))]
    state, token = stats(rate, own, kept, got, jobs, state)
    final, scale = stats(rate, own, kept, got, [([a[4]], (0, 1))], state, is_last=True)

    total_devices = lax.axis_size("dp") * size

    def exchange(array, masks):
        pairs = [[(i, i ^ mask) for i in range(total_devices)] for mask in masks]
        return [array] + [swap(array, pair, ("dp", "ctx")) for pair in pairs]

    def hop(step, parts, arrived, scales=()):
        out = jax.ShapeDtypeStruct((2, 2 * ROWS + (32 if step > 1 else 0), width), BF16)
        return call(
            functools.partial(hop_body, step, len(scales)),
            [out, out, SMALL],
            [],
            1024,
            2 << 20,
            [vmem] * (2 + len(arrived) + len(scales)),
        )(*parts, *arrived, *scales)

    scales = exchange(scale, (4,))
    far, sums = grads(rate, own, kept, got, final, [a[4]])
    from_even = swap(far.astype(BF16), even)
    part_a, part_b, sums = grads(rate, own, kept, got, final, [a[3], b[3]], sums)
    to_a, to_b, scale = hop(3, (part_a, part_b), (from_even,), scales)
    sent_a, sent_b = swap(to_a, even), swap(to_b, odd)
    part_a, part_b, near, sums = grads(rate, own, kept, got, final, [a[2], b[2], own], sums)
    to_a, to_b, beside = hop(2, (part_a, part_b), (sent_a, sent_b))
    sent_a, sent_b = swap(to_a, even), swap(to_b, odd)
    part_a, part_b, query_kept, query_sent = grads(
        rate, own, kept, got, final, [a[1], b[1]], sums, is_last=True
    )
    query_got = swap(query_sent, across)
    to_a, to_b, scale = hop(1, (part_a, part_b), (sent_a, sent_b), [scale, beside])
    sent_a, sent_b = swap(to_a, even), swap(to_b, odd)
    scales = exchange(scale, (8,))
    scales = exchange(scales[0] + scales[1], (64, 128, 192))
    ours, theirs, scale = call(
        last_hop_body,
        [jax.ShapeDtypeStruct((2 * ROWS, width), BF16)] * 2 + [SMALL],
        [],
        1024,
        2 << 20,
        [vmem] * 7,
    )(near, sent_a, sent_b, *scales)
    other = swap(theirs, across)
    scales = exchange(scale, (16, 32, 48))
    query_out, key_out, value_out, scale_out = call(
        finish_body,
        [
            jax.ShapeDtypeStruct((ROWS, 2 * HEADS * HEAD), BF16),
            jax.ShapeDtypeStruct((ROWS, 2 * width), BF16),
            jax.ShapeDtypeStruct((ROWS, 2 * width), BF16),
            jax.ShapeDtypeStruct((1, 2 * HEADS), F32),
        ],
        [],
        1024,
        2 << 20,
        [smem] + [vmem] * 8,
    )(x_ref, query_kept, query_got, ours, other, *scales)
    return query_out[None], key_out[None], value_out[None], scale_out.reshape(2 * HEADS)


def solution(mesh):
    in_specs = (
        P("dp", "ctx", None),
        P("dp", "ctx", None),
        P("dp", "ctx", None),
        P("dp", "ctx", None),
        P("dp", "ctx"),
        P(),
    )
    out_specs = (P("dp", "ctx", None), P("dp", "ctx", None), P("dp", "ctx", None), P())
    return jax.shard_map(local, mesh=mesh, in_specs=in_specs, out_specs=out_specs, check_vma=False)
```

```python
import functools
import math

import jax
import jax.numpy as jnp
from jax import lax
from jax.experimental import pallas as pl
from jax.experimental.pallas import tpu as pltpu
from jax.sharding import PartitionSpec as P

F32 = jnp.float32
BF16 = jnp.bfloat16
HEAD = 128
ROWS = 128
KV_HEADS = 2
GROUP = 7
HEADS = KV_HEADS * GROUP
WIDE = GROUP * ROWS
POS = 16
MESSAGE = POS + 2 * ROWS
TILE = 128
FAR = 32768.0
LOW = -1e30
LOG2E = 1.4426950408889634
NT = (((1,), (1,)), ((), ()))
NN = (((1,), (0,)), ((), ()))
TN = (((0,), (0,)), ((), ()))


def product(a, b, dims):
    return lax.dot_general(a, b, dims, preferred_element_type=F32)


def call(body, outs, scratch, flops, moved, operands, limit=10, aliases=None):
    return pl.pallas_call(
        body,
        out_shape=outs,
        in_specs=operands,
        scratch_shapes=scratch,
        input_output_aliases=aliases or {},
        cost_estimate=pl.CostEstimate(
            flops=flops, bytes_accessed=moved, transcendentals=flops // 1024
        ),
        compiler_params=pltpu.CompilerParams(vmem_limit_bytes=limit * 1024 * 1024),
    )


def fetch(sources, targets, sem):
    copies = [
        pltpu.make_async_copy(source, target, sem.at[n])
        for n, (source, target) in enumerate(zip(sources, targets))
    ]
    for copy in copies:
        copy.start()
    for copy in copies:
        copy.wait()


def pack_keys_body(x_ref, key_in, value_in, pos_in, keep_ref, send_ref, key_ref, value_ref, pos_ref, sem):
    x = x_ref[0]
    fetch((key_in, value_in, pos_in), (key_ref, value_ref, pos_ref), sem)
    pos = pos_ref[...]
    dead = pos < 0
    high = jnp.where(dead, 256, pos >> 7)
    low = jnp.where(dead, 0, pos & 127)
    row = jnp.concatenate([high, low], axis=1).astype(F32)
    rows = jnp.broadcast_to(row, (POS, 2 * ROWS)).astype(BF16)
    for ref, half in ((keep_ref, x), (send_ref, 1 - x)):
        at = pl.multiple_of(half * KV_HEADS * HEAD, KV_HEADS * HEAD)
        ref[0:POS, :] = rows
        ref[POS : POS + ROWS, :] = key_ref[:, pl.ds(at, KV_HEADS * HEAD)]
        ref[POS + ROWS : MESSAGE, :] = value_ref[:, pl.ds(at, KV_HEADS * HEAD)]


def pack_queries_body(x_ref, after_ref, query_in, grad_in, keep_ref, send_ref, query_ref, grad_ref, sem):
    x = x_ref[0]
    fetch((query_in, grad_in), (query_ref, grad_ref), sem)
    for ref, half in ((send_ref, 1 - x), (keep_ref, x)):
        for number, source in enumerate((query_ref, grad_ref)):
            for head in range(HEADS):
                at = pl.multiple_of(half * HEADS * HEAD + head * HEAD, HEAD)
                ref[number, head * ROWS : (head + 1) * ROWS, :] = source[:, pl.ds(at, HEAD)]


def join_body(after_ref, keep_ref, got_ref, out_ref):
    out_ref[0] = keep_ref[...]
    out_ref[1] = got_ref[...]


def finish_body(
    x_ref,
    keep_ref,
    got_ref,
    own_ref,
    other_ref,
    *refs,
):
    scale_refs, (query_out, key_out, value_out, scale_out) = refs[:4], refs[4:]
    x = x_ref[0]
    scale = four([ref[...] for ref in scale_refs])
    scale_out[...] = scale[0:1, : 2 * HEADS]
    for ref, half in ((own_ref, x), (other_ref, 1 - x)):
        at = pl.multiple_of(half * KV_HEADS * HEAD, KV_HEADS * HEAD)
        key_out[:, pl.ds(at, KV_HEADS * HEAD)] = ref[:ROWS, :]
        value_out[:, pl.ds(at, KV_HEADS * HEAD)] = ref[ROWS : 2 * ROWS, :]
    for ref, half in ((keep_ref, x), (got_ref, 1 - x)):
        for head in range(HEADS):
            at = pl.multiple_of(half * HEADS * HEAD + head * HEAD, HEAD)
            query_out[:, pl.ds(at, HEAD)] = ref[head * ROWS : (head + 1) * ROWS, :]


def positions(ref, slot):
    row = ref[slot, 0:POS, :].astype(F32)[0:1, :]
    return row[:, :ROWS] * 128.0 + row[:, ROWS:]


def query_side(own_ref):
    rows = [positions(own_ref, slot) for slot in range(2)]
    rows = [jnp.where(row >= FAR, -1.0, row) for row in rows]
    tops = [jnp.max(row) for row in rows]
    first = jnp.where(tops[0] < tops[1], 0, 1)
    return rows, tops, first


def four(parts):
    return (parts[0] + parts[1]) + (parts[2] + parts[3])


def code(value):
    high = value.astype(BF16)
    value = value - high.astype(F32)
    middle = value.astype(BF16)
    return [high, middle, (value - middle.astype(F32)).astype(BF16)]


def put_scale(ref, scale):
    for number, part in enumerate(code(scale)):
        lanes = slice(0, ROWS) if number < 2 else slice(ROWS, 2 * ROWS)
        rows = jnp.concatenate([part] * 2, axis=0)
        at = 2 * ROWS + (number % 2) * 16
        ref[at : at + 16, lanes] = rows
    ref[2 * ROWS + 16 : 2 * ROWS + 32, ROWS : 2 * ROWS] = jnp.zeros((16, ROWS), BF16)


def get_scale(ref):
    at = 2 * ROWS
    high = ref[at : at + 16, :ROWS].astype(F32)
    middle = ref[at + 16 : at + 32, :ROWS].astype(F32)
    low = ref[at : at + 16, ROWS:].astype(F32)
    return ((high + middle) + low)[0:8]


def hop_body(step, count, *refs):
    part_a, part_b, sent_a = refs[:3]
    refs = refs[3:]
    if step < 3:
        sent_b, refs = refs[0], refs[1:]
    scale_refs, (to_a, to_b, scale_out) = refs[:count], refs[count:]
    plain = slice(0, 2 * ROWS)
    for slot in range(2):
        first = part_a[slot]
        if step < 3:
            first = first + sent_b[slot, plain, :].astype(F32)
        to_a[slot, plain, :] = first.astype(BF16)
        second = part_b[slot] + sent_a[slot, plain, :].astype(F32)
        to_b[slot, plain, :] = second.astype(BF16)
    parts = [ref[...] for ref in scale_refs]
    if step == 3:
        scale = parts[0] + parts[1]
        put_scale(to_a.at[0], scale)
        put_scale(to_b.at[0], scale)
    elif step == 2:
        other = get_scale(sent_b.at[0])
        scale = get_scale(sent_a.at[0]) + other
        put_scale(to_a.at[0], other)
        put_scale(to_b.at[0], other)
    else:
        scale = (parts[0] + get_scale(sent_a.at[0])) + parts[1]
    if step > 1:
        for ref in (to_a, to_b):
            ref[1, 2 * ROWS :, :] = jnp.zeros((32, 2 * ROWS), BF16)
    scale_out[...] = scale


def last_hop_body(near, sent_a, sent_b, *refs):
    scale_refs, (ours, theirs, scale_out) = refs[:4], refs[4:]
    first = near[0] + sent_a[0].astype(F32) + sent_b[0].astype(F32)
    ours[...] = first.astype(BF16)
    second = near[1] + sent_a[1].astype(F32) + sent_b[1].astype(F32)
    theirs[...] = second.astype(BF16)
    scale_out[...] = four([ref[...] for ref in scale_refs])


def place(blocks, first, top, key_c, value_c, pos_c, span=TILE):
    start = jnp.int32(0)
    entries = []
    for phase in range(2):
        slot = first if phase == 0 else 1 - first
        rows = [positions(ref, slot) for ref in blocks]
        begins = [jnp.min(row) for row in rows]
        counts = [jnp.sum(jnp.where(row < FAR, 1.0, 0.0)).astype(jnp.int32) for row in rows]
        counts = [jnp.where(begin <= top, n, 0) for begin, n in zip(begins, counts)]
        chunks = [(n + 15) >> 4 for n in counts]
        def put(number, at, slot=slot, rows=rows):
            ref = blocks[number]
            target = pl.ds(pl.multiple_of(at, 16), ROWS)
            pos_c[target, :] = jnp.broadcast_to(rows[number], (ROWS, ROWS)).T
            for g in range(KV_HEADS):
                lanes = slice(g * HEAD, (g + 1) * HEAD)
                key_c[g, target, :] = ref[slot, POS : POS + ROWS, lanes]
                value_c[g, target, :] = ref[slot, POS + ROWS : MESSAGE, lanes]

        if len(blocks) == 2:
            ahead = begins[0] < begins[1]
            starts = [
                start + jnp.where(ahead, 0, chunks[1] * 16),
                start + jnp.where(ahead, chunks[0] * 16, 0),
            ]

            @pl.when(ahead)
            def _():
                put(0, starts[0])
                put(1, starts[1])

            @pl.when(jnp.logical_not(ahead))
            def _():
                put(1, starts[1])
                put(0, starts[0])

        else:
            starts = []
            total = start
            for number, chunk in enumerate(chunks):
                starts.append(total)
                put(number, total)
                total = total + chunk * 16
        entries.append((slot, starts, counts))
        start = start + sum(chunks) * 16
    rest = pl.ds(pl.multiple_of(start, 16), span)
    pos_c[rest, :] = jnp.full((span, ROWS), 1e9, F32)
    for g in range(KV_HEADS):
        key_c[g, rest, :] = jnp.zeros((span, HEAD), BF16)
        value_c[g, rest, :] = jnp.zeros((span, HEAD), BF16)
    return start, entries


def tile_of(blocks):
    return 2 * TILE if len(blocks) > 2 else TILE


def stats_tile(rate_ref, work_ref, state, key_c, value_c, mask, rows, slot, g):
    some = slice(g * WIDE, (g + 1) * WIDE)
    raw = product(key_c[g, rows, :], work_ref[0, some, :], NT)
    dots = product(value_c[g, rows, :], work_ref[1, some, :], NT)
    for head in range(GROUP):
        lanes = slice(head * ROWS, (head + 1) * ROWS)
        scores = jnp.where(mask, raw[:, lanes] * rate_ref[g, 0:1, lanes], LOW)
        held = [state[slot * KV_HEADS + g, n, :, lanes] for n in range(5)]
        top, total, weighted, shifted, both = held
        scores = scores.reshape(mask.shape[0] // 8, 8, ROWS)
        new_top = jnp.maximum(top, jnp.max(scores, axis=0))
        above = scores - new_top[None]
        weights = jnp.exp2(above)
        weighted_dots = weights * dots[:, lanes].reshape(mask.shape[0] // 8, 8, ROWS)
        step_down = top - new_top
        factor = jnp.exp2(step_down)
        held = [
            new_top,
            factor * total + jnp.sum(weights, axis=0),
            factor * weighted + jnp.sum(weighted_dots, axis=0),
            factor * (shifted + step_down * total) + jnp.sum(weights * above, axis=0),
            factor * (both + step_down * weighted) + jnp.sum(weighted_dots * above, axis=0),
        ]
        for n in range(5):
            state[slot * KV_HEADS + g, n, :, lanes] = held[n]


def stats_body(jobs, is_first, is_last, *refs):
    rate_ref, own_ref, kept_ref, got_ref = refs[:4]
    refs = refs[4:]
    work = []
    for count, slots in jobs:
        work.append((refs[:count], slots))
        refs = refs[count:]
    if not is_first:
        prior_ref, refs = refs[0], refs[1:]
    if is_last:
        final_ref, scale_ref, far_ref, query_sum, state, key_c, value_c, pos_c = refs[:8]
        key_sum, value_sum = refs[8:]
    else:
        state, token_ref, key_c, value_c, pos_c = refs
        token_ref[...] = jnp.zeros_like(token_ref)
    query_rows, tops, first = query_side(own_ref)
    if is_first:
        state[...] = jnp.zeros_like(state)
        state[:, 0] = jnp.full((2 * KV_HEADS, 8, WIDE), LOW, F32)
    else:
        state[...] = prior_ref[...]
    for blocks, slots in work:
        span = tile_of(blocks)
        top = jnp.maximum(tops[0], tops[1]) if len(slots) == 2 else tops[slots[0]]
        length, entries = place(blocks, first, top, key_c, value_c, pos_c, span)

        def tile(step, _, slots=slots, span=span):
            at = pl.multiple_of(step * span, span)
            key_pos = pos_c[pl.ds(at, span), :]
            lowest = jnp.min(key_pos)
            for slot in slots:

                @pl.when(lowest <= tops[slot])
                def _(slot=slot):
                    mask = key_pos <= query_rows[slot]
                    for g in range(KV_HEADS):
                        stats_tile(
                            rate_ref,
                            (kept_ref, got_ref)[slot],
                            state,
                            key_c,
                            value_c,
                            mask,
                            pl.ds(at, span),
                            slot,
                            g,
                        )

            return 0

        lax.fori_loop(0, (length + span - 1) // span, tile, 0)
    if not is_last:
        return
    lane = lax.broadcasted_iota(jnp.int32, (8, ROWS), 1)
    scale_row = jnp.zeros((8, ROWS), F32)
    for slot in range(2):
        live = query_rows[slot] >= 0.0
        for g in range(KV_HEADS):
            for head in range(GROUP):
                lanes = slice(head * ROWS, (head + 1) * ROWS)
                held = [state[slot * KV_HEADS + g, n, :, lanes] for n in range(5)]
                tops_in, total, weighted, shifted, both = held
                top = jnp.max(tops_in, axis=0, keepdims=True)
                step_down = tops_in - top
                factor = jnp.exp2(step_down)
                both = jnp.sum(factor * (both + step_down * weighted), axis=0, keepdims=True)
                shifted = jnp.sum(factor * (shifted + step_down * total), axis=0, keepdims=True)
                weighted = jnp.sum(factor * weighted, axis=0, keepdims=True)
                total = jnp.sum(factor * total, axis=0, keepdims=True)
                total = jnp.where(live, total, 1.0)
                mean = weighted / total
                spread = (both - mean * shifted) / total
                rate = rate_ref[g, 0:1, lanes] * math.sqrt(HEAD)
                spread = jnp.where(live, spread / rate, 0.0)
                final_ref[slot * KV_HEADS + g, 0:2, lanes] = jnp.concatenate(
                    [
                        jnp.where(live, top + jnp.log2(total), -LOW),
                        jnp.where(live, mean, 0.0),
                    ],
                    axis=0,
                )
                place_at = first * HEADS + g * GROUP + head
                scale_row = scale_row + jnp.where(
                    lane == place_at, jnp.sum(spread, axis=1, keepdims=True), 0.0
                )
    scale_ref[...] = scale_row
    query_sum[...] = jnp.zeros_like(query_sum)
    grads_work(
        rate_ref,
        (kept_ref, got_ref),
        final_ref,
        key_c,
        value_c,
        pos_c,
        key_sum,
        value_sum,
        query_sum,
        query_rows,
        tops,
        length,
        entries,
        [far_ref],
    )


def grads_tile(
    rate_ref,
    work_ref,
    final_ref,
    key_c,
    value_c,
    key_sum,
    value_sum,
    query_sum,
    mask,
    at,
    slot,
    g,
):
    some = slice(g * WIDE, (g + 1) * WIDE)
    rows = pl.ds(at, TILE)
    keys = key_c[g, rows, :]
    values = value_c[g, rows, :]
    queries = work_ref[0, some, :]
    gradients = work_ref[1, some, :]
    raw = product(keys, queries, NT)
    dots = product(values, gradients, NT)
    probs, score_grads = [], []
    for head in range(GROUP):
        lanes = slice(head * ROWS, (head + 1) * ROWS)
        rate = rate_ref[g, 0:1, lanes]
        held = final_ref[slot * KV_HEADS + g, :, lanes]
        prob = jnp.where(mask, jnp.exp2(raw[:, lanes] * rate - held[0:1]), 0.0)
        grad = prob * (dots[:, lanes] - held[1:2])
        probs.append(prob.astype(BF16))
        score_grads.append((grad * (rate * (1.0 / LOG2E))).astype(BF16))
    prob_low = jnp.concatenate(probs, axis=1)
    score_low = jnp.concatenate(score_grads, axis=1)
    value_sum[g, rows, :] += product(prob_low, gradients, NN)
    key_sum[g, rows, :] += product(score_low, queries, NN)
    query_sum[slot * KV_HEADS + g] += product(keys, score_low, TN)


def grads_work(
    rate_ref,
    work_refs,
    final_ref,
    key_c,
    value_c,
    pos_c,
    key_sum,
    value_sum,
    query_sum,
    query_rows,
    tops,
    length,
    entries,
    outs,
):
    def tile(step, _):
        at = pl.multiple_of(step * TILE, TILE)
        key_pos = pos_c[pl.ds(at, TILE), :]
        lowest = jnp.min(key_pos)
        for g in range(KV_HEADS):
            key_sum[g, pl.ds(at, TILE), :] = jnp.zeros((TILE, HEAD), F32)
            value_sum[g, pl.ds(at, TILE), :] = jnp.zeros((TILE, HEAD), F32)
        for slot in range(2):

            @pl.when(lowest <= tops[slot])
            def _(slot=slot):
                mask = key_pos <= query_rows[slot]
                for g in range(KV_HEADS):
                    grads_tile(
                        rate_ref,
                        work_refs[slot],
                        final_ref,
                        key_c,
                        value_c,
                        key_sum,
                        value_sum,
                        query_sum,
                        mask,
                        at,
                        slot,
                        g,
                    )

        return 0

    lax.fori_loop(0, (length + TILE - 1) // TILE, tile, 0)
    row = lax.broadcasted_iota(jnp.int32, (ROWS, HEAD), 0)
    for slot, starts, counts in entries:
        for out, at, n in zip(outs, starts, counts):
            at = pl.multiple_of(at, 16)
            for g in range(KV_HEADS):
                lanes = slice(g * HEAD, (g + 1) * HEAD)
                for number, total in enumerate((key_sum, value_sum)):
                    out[slot, number * ROWS : (number + 1) * ROWS, lanes] = jnp.where(
                        row < n, total[g, pl.ds(at, ROWS), :], 0.0
                    )


def grads_body(count, is_first, is_last, *refs):
    rate_ref, own_ref, kept_ref, got_ref, final_ref = refs[:5]
    blocks = refs[5 : 5 + count]
    refs = refs[5 + count :]
    if not is_first:
        prior_ref, refs = refs[0], refs[1:]
    outs, refs = refs[:count], refs[count:]
    if is_last:
        query_outs, refs = refs[:2], refs[2:]
    query_sum, key_c, value_c, pos_c, key_sum, value_sum = refs
    query_rows, tops, first = query_side(own_ref)
    length, entries = place(
        blocks, first, jnp.maximum(tops[0], tops[1]), key_c, value_c, pos_c
    )
    if is_first:
        query_sum[...] = jnp.zeros_like(query_sum)
    elif is_last:
        query_sum[...] = prior_ref[...]

    grads_work(
        rate_ref,
        (kept_ref, got_ref),
        final_ref,
        key_c,
        value_c,
        pos_c,
        key_sum,
        value_sum,
        query_sum,
        query_rows,
        tops,
        length,
        entries,
        outs,
    )
    if is_last:
        for slot in range(2):
            for g in range(KV_HEADS):
                for head in range(GROUP):
                    lanes = slice(head * ROWS, (head + 1) * ROWS)
                    rows = slice((g * GROUP + head) * ROWS, (g * GROUP + head + 1) * ROWS)
                    query_outs[slot][rows, :] = query_sum[slot * KV_HEADS + g, :, lanes].T.astype(
                        BF16
                    )


def compact_scratch(count):
    size = 2 * count * ROWS + 2 * TILE
    return [
        pltpu.VMEM((KV_HEADS, size, HEAD), BF16),
        pltpu.VMEM((KV_HEADS, size, HEAD), BF16),
        pltpu.VMEM((size, ROWS), F32),
    ]


STATE = jax.ShapeDtypeStruct((2 * KV_HEADS, 5, 8, WIDE), F32)
PART = jax.ShapeDtypeStruct((2, 2 * ROWS, KV_HEADS * HEAD), F32)
SUMS = jax.ShapeDtypeStruct((2 * KV_HEADS, HEAD, WIDE), F32)
SMALL = jax.ShapeDtypeStruct((8, ROWS), F32)
FINAL = jax.ShapeDtypeStruct((2 * KV_HEADS, 8, WIDE), F32)


def stats(rate, own, kept, got, jobs, prior=None, is_last=False):
    if is_last:
        outs = [FINAL, SMALL, PART, SUMS]
        scratch = [pltpu.VMEM(STATE.shape, F32)]
    else:
        outs, scratch = [STATE, SMALL], []
    blocks = [block for some, _ in jobs for block in some]
    operands = [rate, own, kept, got, *blocks] + ([] if prior is None else [prior])
    sizes = [(len(some), slots) for some, slots in jobs]
    rest = []
    if is_last:
        size = 2 * ROWS + TILE
        rest = [pltpu.VMEM((KV_HEADS, size, HEAD), F32), pltpu.VMEM((KV_HEADS, size, HEAD), F32)]
    return call(
        functools.partial(stats_body, sizes, prior is None, is_last),
        outs,
        scratch + compact_scratch(max(count for count, _ in sizes)) + rest,
        sum(count * len(slots) for count, slots in sizes) * ROWS * 2 * HEADS * ROWS * HEAD * 4,
        4 << 20,
        [pl.BlockSpec(memory_space=pltpu.VMEM)] * len(operands),
    )(*operands)


def grads(rate, own, kept, got, final, blocks, prior=None, is_last=False):
    count = len(blocks)
    outs = [jax.ShapeDtypeStruct((2, 2 * ROWS, KV_HEADS * HEAD), F32)] * count
    sums = jax.ShapeDtypeStruct((2 * KV_HEADS, HEAD, WIDE), F32)
    operands = [rate, own, kept, got, final, *blocks]
    operands = operands + ([] if prior is None else [prior])
    if is_last:
        outs = outs + [jax.ShapeDtypeStruct((HEADS * ROWS, HEAD), BF16)] * 2
        scratch = [pltpu.VMEM(sums.shape, F32)]
    else:
        outs, scratch = outs + [sums], []
    aliases = {} if prior is None or is_last else {len(operands) - 1: len(outs) - 1}
    size = 2 * count * ROWS + TILE
    scratch = (
        scratch
        + compact_scratch(count)
        + [pltpu.VMEM((KV_HEADS, size, HEAD), F32), pltpu.VMEM((KV_HEADS, size, HEAD), F32)]
    )
    return call(
        functools.partial(grads_body, count, prior is None, is_last),
        outs,
        scratch,
        count * 2 * ROWS * 2 * HEADS * ROWS * 2 * HEAD * 5,
        6 << 20,
        [pl.BlockSpec(memory_space=pltpu.VMEM)] * len(operands),
        aliases=aliases,
    )(*operands)


def local(queries, keys, values, out_grad, routes, per_head_scale):
    me = lax.axis_index("ctx")
    size = lax.axis_size("ctx")
    ring = size // 2
    x = (me // ring).astype(jnp.int32)
    x_ref = x.reshape(1)
    across = [(i, (i + ring) % size) for i in range(size)]

    def neighbour(i, up):
        base, z = i // ring * ring, i % ring
        return base + (z + (1 if up == (z % 2 == 0) else -1)) % ring

    even = [(i, neighbour(i, True)) for i in range(size)]
    odd = [(i, neighbour(i, False)) for i in range(size)]

    def swap(array, pairs, axis="ctx"):
        return lax.ppermute(array, axis, pairs)

    smem = pl.BlockSpec(memory_space=pltpu.SMEM)
    vmem = pl.BlockSpec(memory_space=pltpu.VMEM)
    anywhere = pl.BlockSpec(memory_space=pl.ANY)
    in_hbm = pl.BlockSpec(memory_space=pltpu.HBM)
    width = KV_HEADS * HEAD
    message = jax.ShapeDtypeStruct((MESSAGE, width), BF16)
    keys_kept, keys_sent = call(
        pack_keys_body,
        [message, message],
        [
            pltpu.VMEM((ROWS, 2 * width), BF16),
            pltpu.VMEM((ROWS, 2 * width), BF16),
            pltpu.VMEM((1, ROWS), jnp.int32),
            pltpu.SemaphoreType.DMA((3,)),
        ],
        1024,
        1 << 20,
        [smem, in_hbm, in_hbm, in_hbm],
        60,
    )(x_ref, keys[0], values[0], routes)
    keys_got = swap(keys_sent, across)
    work = jax.ShapeDtypeStruct((2, HEADS * ROWS, HEAD), BF16)
    kept, sent = call(
        pack_queries_body,
        [work, work],
        [
            pltpu.VMEM((ROWS, 2 * HEADS * HEAD), BF16),
            pltpu.VMEM((ROWS, 2 * HEADS * HEAD), BF16),
            pltpu.SemaphoreType.DMA((2,)),
        ],
        1024,
        4 << 20,
        [smem, anywhere, in_hbm, in_hbm],
        60,
    )(x_ref, keys_sent, queries[0], out_grad[0])
    got = swap(sent, across)
    own = call(
        join_body,
        jax.ShapeDtypeStruct((2, MESSAGE, width), BF16),
        [],
        1024,
        1 << 20,
        [anywhere, vmem, vmem],
    )(sent, keys_kept, keys_got)

    half_scale = lax.dynamic_slice_in_dim(per_head_scale, x * HEADS, HEADS)
    rate = jnp.repeat(half_scale * (LOG2E / math.sqrt(HEAD)), ROWS).reshape(KV_HEADS, 1, WIDE)
    rate = jnp.broadcast_to(rate, (KV_HEADS, 8, WIDE))

    def gate(blocks, after):
        def body(*refs):
            for source, target in zip(refs, refs[len(blocks) + 1 :]):
                target[...] = source[...]

        return call(
            body,
            [jax.ShapeDtypeStruct(block.shape, block.dtype) for block in blocks],
            [],
            1024,
            1 << 20,
            [vmem] * (len(blocks) + 1),
        )(*blocks, after)

    a, b = [own], [own]
    a.append(swap(own, even))
    b.append(swap(own, odd))
    state, token = stats(rate, own, kept, kept, [([own], (0,))])
    a[1], b[1] = gate([a[1], b[1]], token)
    a.append(swap(b[1], even))
    b.append(swap(a[1], odd))
    state, token = stats(rate, own, kept, kept, [([a[1], b[1]], (0,))], state)
    a[2], b[2] = gate([a[2], b[2]], token)
    a.append(swap(b[2], even))
    b.append(swap(a[2], odd))
    state, token = stats(rate, own, kept, kept, [([a[2], b[2]], (0,))], state)
    a[3], b[3] = gate([a[3], b[3]], token)
    a.append(swap(b[3], even))
    jobs = [([own, a[1], b[1], a[2], b[2]], (1,)), ([a[3], b[3]], (0, 1))]
    state, token = stats(rate, own, kept, got, jobs, state)
    final, scale, far, sums = stats(rate, own, kept, got, [([a[4]], (0, 1))], state, is_last=True)

    total_devices = lax.axis_size("dp") * size

    def exchange(array, masks):
        pairs = [[(i, i ^ mask) for i in range(total_devices)] for mask in masks]
        return [array] + [swap(array, pair, ("dp", "ctx")) for pair in pairs]

    def hop(step, parts, arrived, scales=()):
        out = jax.ShapeDtypeStruct((2, 2 * ROWS + (32 if step > 1 else 0), width), BF16)
        return call(
            functools.partial(hop_body, step, len(scales)),
            [out, out, SMALL],
            [],
            1024,
            2 << 20,
            [vmem] * (2 + len(arrived) + len(scales)),
        )(*parts, *arrived, *scales)

    scales = exchange(scale, (4,))
    from_even = swap(far.astype(BF16), even)
    part_a, part_b, sums = grads(rate, own, kept, got, final, [a[3], b[3]], sums)
    to_a, to_b, scale = hop(3, (part_a, part_b), (from_even,), scales)
    sent_a, sent_b = swap(to_a, even), swap(to_b, odd)
    part_a, part_b, near, sums = grads(rate, own, kept, got, final, [a[2], b[2], own], sums)
    to_a, to_b, beside = hop(2, (part_a, part_b), (sent_a, sent_b))
    sent_a, sent_b = swap(to_a, even), swap(to_b, odd)
    part_a, part_b, query_kept, query_sent = grads(
        rate, own, kept, got, final, [a[1], b[1]], sums, is_last=True
    )
    query_got = swap(query_sent, across)
    to_a, to_b, scale = hop(1, (part_a, part_b), (sent_a, sent_b), [scale, beside])
    sent_a, sent_b = swap(to_a, even), swap(to_b, odd)
    scales = exchange(scale, (8,))
    scales = exchange(scales[0] + scales[1], (64, 128, 192))
    ours, theirs, scale = call(
        last_hop_body,
        [jax.ShapeDtypeStruct((2 * ROWS, width), BF16)] * 2 + [SMALL],
        [],
        1024,
        2 << 20,
        [vmem] * 7,
    )(near, sent_a, sent_b, *scales)
    other = swap(theirs, across)
    scales = exchange(scale, (16, 32, 48))
    query_out, key_out, value_out, scale_out = call(
        finish_body,
        [
            jax.ShapeDtypeStruct((ROWS, 2 * HEADS * HEAD), BF16),
            jax.ShapeDtypeStruct((ROWS, 2 * width), BF16),
            jax.ShapeDtypeStruct((ROWS, 2 * width), BF16),
            jax.ShapeDtypeStruct((1, 2 * HEADS), F32),
        ],
        [],
        1024,
        2 << 20,
        [smem] + [vmem] * 8,
    )(x_ref, query_kept, query_got, ours, other, *scales)
    return query_out[None], key_out[None], value_out[None], scale_out.reshape(2 * HEADS)


def solution(mesh):
    in_specs = (
        P("dp", "ctx", None),
        P("dp", "ctx", None),
        P("dp", "ctx", None),
        P("dp", "ctx", None),
        P("dp", "ctx"),
        P(),
    )
    out_specs = (P("dp", "ctx", None), P("dp", "ctx", None), P("dp", "ctx", None), P())
    return jax.shard_map(local, mesh=mesh, in_specs=in_specs, out_specs=out_specs, check_vma=False)
```

```python
import functools
import math

import jax
import jax.numpy as jnp
from jax import lax
from jax.experimental import pallas as pl
from jax.experimental.pallas import tpu as pltpu
from jax.sharding import PartitionSpec as P

F32 = jnp.float32
BF16 = jnp.bfloat16
HEAD = 128
ROWS = 128
KV_HEADS = 2
GROUP = 7
HEADS = KV_HEADS * GROUP
WIDE = GROUP * ROWS
POS = 16
MESSAGE = POS + 2 * ROWS
TILE = 128
FAR = 32768.0
LOW = -1e30
LOG2E = 1.4426950408889634
NT = (((1,), (1,)), ((), ()))
NN = (((1,), (0,)), ((), ()))
TN = (((0,), (0,)), ((), ()))


def product(a, b, dims):
    return lax.dot_general(a, b, dims, preferred_element_type=F32)


def call(body, outs, scratch, flops, moved, operands, limit=10, aliases=None):
    return pl.pallas_call(
        body,
        out_shape=outs,
        in_specs=operands,
        scratch_shapes=scratch,
        input_output_aliases=aliases or {},
        cost_estimate=pl.CostEstimate(
            flops=flops, bytes_accessed=moved, transcendentals=flops // 1024
        ),
        compiler_params=pltpu.CompilerParams(vmem_limit_bytes=limit * 1024 * 1024),
    )


def fetch(sources, targets, sem):
    copies = [
        pltpu.make_async_copy(source, target, sem.at[n])
        for n, (source, target) in enumerate(zip(sources, targets))
    ]
    for copy in copies:
        copy.start()
    for copy in copies:
        copy.wait()


def pack_keys_body(x_ref, key_in, value_in, pos_in, keep_ref, send_ref, key_ref, value_ref, pos_ref, sem):
    x = x_ref[0]
    fetch((key_in, value_in, pos_in), (key_ref, value_ref, pos_ref), sem)
    pos = pos_ref[...]
    dead = pos < 0
    high = jnp.where(dead, 256, pos >> 7)
    low = jnp.where(dead, 0, pos & 127)
    row = jnp.concatenate([high, low], axis=1).astype(F32)
    rows = jnp.broadcast_to(row, (POS, 2 * ROWS)).astype(BF16)
    for ref, half in ((keep_ref, x), (send_ref, 1 - x)):
        at = pl.multiple_of(half * KV_HEADS * HEAD, KV_HEADS * HEAD)
        ref[0:POS, :] = rows
        ref[POS : POS + ROWS, :] = key_ref[:, pl.ds(at, KV_HEADS * HEAD)]
        ref[POS + ROWS : MESSAGE, :] = value_ref[:, pl.ds(at, KV_HEADS * HEAD)]


def pack_queries_body(x_ref, after_ref, query_in, grad_in, keep_ref, send_ref, query_ref, grad_ref, sem):
    x = x_ref[0]
    fetch((query_in, grad_in), (query_ref, grad_ref), sem)
    for ref, half in ((send_ref, 1 - x), (keep_ref, x)):
        for number, source in enumerate((query_ref, grad_ref)):
            for head in range(HEADS):
                at = pl.multiple_of(half * HEADS * HEAD + head * HEAD, HEAD)
                ref[number, head * ROWS : (head + 1) * ROWS, :] = source[:, pl.ds(at, HEAD)]


def join_body(after_ref, keep_ref, got_ref, out_ref):
    out_ref[0] = keep_ref[...]
    out_ref[1] = got_ref[...]


def finish_body(
    x_ref,
    keep_ref,
    got_ref,
    own_ref,
    other_ref,
    *refs,
):
    scale_refs, (query_out, key_out, value_out, scale_out) = refs[:4], refs[4:]
    x = x_ref[0]
    scale = four([ref[...] for ref in scale_refs])
    scale_out[...] = scale[0:1, : 2 * HEADS]
    for ref, half in ((own_ref, x), (other_ref, 1 - x)):
        at = pl.multiple_of(half * KV_HEADS * HEAD, KV_HEADS * HEAD)
        key_out[:, pl.ds(at, KV_HEADS * HEAD)] = ref[:ROWS, :]
        value_out[:, pl.ds(at, KV_HEADS * HEAD)] = ref[ROWS : 2 * ROWS, :]
    for ref, half in ((keep_ref, x), (got_ref, 1 - x)):
        for head in range(HEADS):
            at = pl.multiple_of(half * HEADS * HEAD + head * HEAD, HEAD)
            query_out[:, pl.ds(at, HEAD)] = ref[head * ROWS : (head + 1) * ROWS, :]


def positions(ref, slot):
    row = ref[slot, 0:POS, :].astype(F32)[0:1, :]
    return row[:, :ROWS] * 128.0 + row[:, ROWS:]


def query_side(own_ref):
    rows = [positions(own_ref, slot) for slot in range(2)]
    rows = [jnp.where(row >= FAR, -1.0, row) for row in rows]
    tops = [jnp.max(row) for row in rows]
    first = jnp.where(tops[0] < tops[1], 0, 1)
    return rows, tops, first


def four(parts):
    return (parts[0] + parts[1]) + (parts[2] + parts[3])


def code(value):
    high = value.astype(BF16)
    value = value - high.astype(F32)
    middle = value.astype(BF16)
    return [high, middle, (value - middle.astype(F32)).astype(BF16)]


def put_scale(ref, scale):
    for number, part in enumerate(code(scale)):
        lanes = slice(0, ROWS) if number < 2 else slice(ROWS, 2 * ROWS)
        rows = jnp.concatenate([part] * 2, axis=0)
        at = 2 * ROWS + (number % 2) * 16
        ref[at : at + 16, lanes] = rows
    ref[2 * ROWS + 16 : 2 * ROWS + 32, ROWS : 2 * ROWS] = jnp.zeros((16, ROWS), BF16)


def get_scale(ref):
    at = 2 * ROWS
    high = ref[at : at + 16, :ROWS].astype(F32)
    middle = ref[at + 16 : at + 32, :ROWS].astype(F32)
    low = ref[at : at + 16, ROWS:].astype(F32)
    return ((high + middle) + low)[0:8]


def hop_body(step, count, *refs):
    part_a, part_b, sent_a = refs[:3]
    refs = refs[3:]
    if step < 3:
        sent_b, refs = refs[0], refs[1:]
    scale_refs, (to_a, to_b, scale_out) = refs[:count], refs[count:]
    plain = slice(0, 2 * ROWS)
    for slot in range(2):
        first = part_a[slot]
        if step < 3:
            first = first + sent_b[slot, plain, :].astype(F32)
        to_a[slot, plain, :] = first.astype(BF16)
        second = part_b[slot] + sent_a[slot, plain, :].astype(F32)
        to_b[slot, plain, :] = second.astype(BF16)
    parts = [ref[...] for ref in scale_refs]
    if step == 3:
        scale = parts[0] + parts[1]
        put_scale(to_a.at[0], scale)
        put_scale(to_b.at[0], scale)
    elif step == 2:
        other = get_scale(sent_b.at[0])
        scale = get_scale(sent_a.at[0]) + other
        put_scale(to_a.at[0], other)
        put_scale(to_b.at[0], other)
    else:
        scale = (parts[0] + get_scale(sent_a.at[0])) + parts[1]
    if step > 1:
        for ref in (to_a, to_b):
            ref[1, 2 * ROWS :, :] = jnp.zeros((32, 2 * ROWS), BF16)
    scale_out[...] = scale


def last_hop_body(near, sent_a, sent_b, *refs):
    scale_refs, (ours, theirs, scale_out) = refs[:4], refs[4:]
    first = near[0] + sent_a[0].astype(F32) + sent_b[0].astype(F32)
    ours[...] = first.astype(BF16)
    second = near[1] + sent_a[1].astype(F32) + sent_b[1].astype(F32)
    theirs[...] = second.astype(BF16)
    scale_out[...] = four([ref[...] for ref in scale_refs])


def place(blocks, first, top, key_c, value_c, pos_c, span=TILE):
    start = jnp.int32(0)
    entries = []
    for phase in range(2):
        slot = first if phase == 0 else 1 - first
        rows = [positions(ref, slot) for ref in blocks]
        begins = [jnp.min(row) for row in rows]
        counts = [jnp.sum(jnp.where(row < FAR, 1.0, 0.0)).astype(jnp.int32) for row in rows]
        counts = [jnp.where(begin <= top, n, 0) for begin, n in zip(begins, counts)]
        chunks = [(n + 15) >> 4 for n in counts]
        def put(number, at, slot=slot, rows=rows):
            ref = blocks[number]
            target = pl.ds(pl.multiple_of(at, 16), ROWS)
            pos_c[target, :] = jnp.broadcast_to(rows[number], (ROWS, ROWS)).T
            for g in range(KV_HEADS):
                lanes = slice(g * HEAD, (g + 1) * HEAD)
                key_c[g, target, :] = ref[slot, POS : POS + ROWS, lanes]
                value_c[g, target, :] = ref[slot, POS + ROWS : MESSAGE, lanes]

        if len(blocks) == 2:
            ahead = begins[0] < begins[1]
            starts = [
                start + jnp.where(ahead, 0, chunks[1] * 16),
                start + jnp.where(ahead, chunks[0] * 16, 0),
            ]

            @pl.when(ahead)
            def _():
                put(0, starts[0])
                put(1, starts[1])

            @pl.when(jnp.logical_not(ahead))
            def _():
                put(1, starts[1])
                put(0, starts[0])

        else:
            starts = []
            total = start
            for number, chunk in enumerate(chunks):
                starts.append(total)
                put(number, total)
                total = total + chunk * 16
        entries.append((slot, starts, counts))
        start = start + sum(chunks) * 16
    rest = pl.ds(pl.multiple_of(start, 16), span)
    pos_c[rest, :] = jnp.full((span, ROWS), 1e9, F32)
    for g in range(KV_HEADS):
        key_c[g, rest, :] = jnp.zeros((span, HEAD), BF16)
        value_c[g, rest, :] = jnp.zeros((span, HEAD), BF16)
    return start, entries


def tile_of(blocks):
    return 2 * TILE if len(blocks) > 2 else TILE


def stats_tile(rate_ref, work_ref, state, key_c, value_c, mask, rows, slot, g):
    some = slice(g * WIDE, (g + 1) * WIDE)
    raw = product(key_c[g, rows, :], work_ref[0, some, :], NT)
    dots = product(value_c[g, rows, :], work_ref[1, some, :], NT)
    for head in range(GROUP):
        lanes = slice(head * ROWS, (head + 1) * ROWS)
        scores = jnp.where(mask, raw[:, lanes] * rate_ref[g, 0:1, lanes], LOW)
        held = [state[slot * KV_HEADS + g, n, :, lanes] for n in range(5)]
        top, total, weighted, shifted, both = held
        scores = scores.reshape(mask.shape[0] // 8, 8, ROWS)
        new_top = jnp.maximum(top, jnp.max(scores, axis=0))
        above = scores - new_top[None]
        weights = jnp.exp2(above)
        weighted_dots = weights * dots[:, lanes].reshape(mask.shape[0] // 8, 8, ROWS)
        step_down = top - new_top
        factor = jnp.exp2(step_down)
        held = [
            new_top,
            factor * total + jnp.sum(weights, axis=0),
            factor * weighted + jnp.sum(weighted_dots, axis=0),
            factor * (shifted + step_down * total) + jnp.sum(weights * above, axis=0),
            factor * (both + step_down * weighted) + jnp.sum(weighted_dots * above, axis=0),
        ]
        for n in range(5):
            state[slot * KV_HEADS + g, n, :, lanes] = held[n]


def stats_body(jobs, is_first, is_last, *refs):
    rate_ref, own_ref, kept_ref, got_ref = refs[:4]
    refs = refs[4:]
    work = []
    for count, slots in jobs:
        work.append((refs[:count], slots))
        refs = refs[count:]
    if not is_first:
        prior_ref, refs = refs[0], refs[1:]
    if is_last:
        final_ref, scale_ref, far_ref, query_sum, state, key_c, value_c, pos_c = refs[:8]
        key_sum, value_sum = refs[8:]
    else:
        state, token_ref, key_c, value_c, pos_c = refs
        token_ref[...] = jnp.zeros_like(token_ref)
    query_rows, tops, first = query_side(own_ref)
    if is_first:
        state[...] = jnp.zeros_like(state)
        state[:, 0] = jnp.full((2 * KV_HEADS, 8, WIDE), LOW, F32)
    else:
        state[...] = prior_ref[...]
    for blocks, slots in work:
        span = tile_of(blocks)
        top = jnp.maximum(tops[0], tops[1]) if len(slots) == 2 else tops[slots[0]]
        length, entries = place(blocks, first, top, key_c, value_c, pos_c, span)

        def tile(step, _, slots=slots, span=span):
            at = pl.multiple_of(step * span, span)
            key_pos = pos_c[pl.ds(at, span), :]
            lowest = jnp.min(key_pos)
            for slot in slots:

                @pl.when(lowest <= tops[slot])
                def _(slot=slot):
                    mask = key_pos <= query_rows[slot]
                    for g in range(KV_HEADS):
                        stats_tile(
                            rate_ref,
                            (kept_ref, got_ref)[slot],
                            state,
                            key_c,
                            value_c,
                            mask,
                            pl.ds(at, span),
                            slot,
                            g,
                        )

            return 0

        lax.fori_loop(0, (length + span - 1) // span, tile, 0)
    if not is_last:
        return
    lane = lax.broadcasted_iota(jnp.int32, (8, ROWS), 1)
    scale_row = jnp.zeros((8, ROWS), F32)
    for slot in range(2):
        live = query_rows[slot] >= 0.0
        for g in range(KV_HEADS):
            for head in range(GROUP):
                lanes = slice(head * ROWS, (head + 1) * ROWS)
                held = [state[slot * KV_HEADS + g, n, :, lanes] for n in range(5)]
                tops_in, total, weighted, shifted, both = held
                top = jnp.max(tops_in, axis=0, keepdims=True)
                step_down = tops_in - top
                factor = jnp.exp2(step_down)
                both = jnp.sum(factor * (both + step_down * weighted), axis=0, keepdims=True)
                shifted = jnp.sum(factor * (shifted + step_down * total), axis=0, keepdims=True)
                weighted = jnp.sum(factor * weighted, axis=0, keepdims=True)
                total = jnp.sum(factor * total, axis=0, keepdims=True)
                total = jnp.where(live, total, 1.0)
                mean = weighted / total
                spread = (both - mean * shifted) / total
                rate = rate_ref[g, 0:1, lanes] * math.sqrt(HEAD)
                spread = jnp.where(live, spread / rate, 0.0)
                final_ref[slot * KV_HEADS + g, 0:2, lanes] = jnp.concatenate(
                    [
                        jnp.where(live, top + jnp.log2(total), -LOW),
                        jnp.where(live, mean, 0.0),
                    ],
                    axis=0,
                )
                place_at = first * HEADS + g * GROUP + head
                scale_row = scale_row + jnp.where(
                    lane == place_at, jnp.sum(spread, axis=1, keepdims=True), 0.0
                )
    scale_ref[...] = scale_row
    query_sum[...] = jnp.zeros_like(query_sum)
    grads_work(
        rate_ref,
        (kept_ref, got_ref),
        final_ref,
        key_c,
        value_c,
        pos_c,
        key_sum,
        value_sum,
        query_sum,
        query_rows,
        tops,
        length,
        entries,
        [far_ref],
    )


def grads_tile(
    rate_ref,
    work_ref,
    final_ref,
    key_c,
    value_c,
    key_sum,
    value_sum,
    query_sum,
    mask,
    at,
    slot,
    g,
):
    some = slice(g * WIDE, (g + 1) * WIDE)
    rows = pl.ds(at, TILE)
    keys = key_c[g, rows, :]
    values = value_c[g, rows, :]
    queries = work_ref[0, some, :]
    gradients = work_ref[1, some, :]
    raw = product(keys, queries, NT)
    dots = product(values, gradients, NT)
    probs, score_grads = [], []
    for head in range(GROUP):
        lanes = slice(head * ROWS, (head + 1) * ROWS)
        rate = rate_ref[g, 0:1, lanes]
        held = final_ref[slot * KV_HEADS + g, :, lanes]
        prob = jnp.where(mask, jnp.exp2(raw[:, lanes] * rate - held[0:1]), 0.0)
        grad = prob * (dots[:, lanes] - held[1:2])
        probs.append(prob.astype(BF16))
        score_grads.append((grad * (rate * (1.0 / LOG2E))).astype(BF16))
    prob_low = jnp.concatenate(probs, axis=1)
    score_low = jnp.concatenate(score_grads, axis=1)
    value_sum[g, rows, :] += product(prob_low, gradients, NN)
    key_sum[g, rows, :] += product(score_low, queries, NN)
    query_sum[slot * KV_HEADS + g] += product(keys, score_low, TN)


def grads_work(
    rate_ref,
    work_refs,
    final_ref,
    key_c,
    value_c,
    pos_c,
    key_sum,
    value_sum,
    query_sum,
    query_rows,
    tops,
    length,
    entries,
    outs,
):
    def tile(step, _):
        at = pl.multiple_of(step * TILE, TILE)
        key_pos = pos_c[pl.ds(at, TILE), :]
        lowest = jnp.min(key_pos)
        for g in range(KV_HEADS):
            key_sum[g, pl.ds(at, TILE), :] = jnp.zeros((TILE, HEAD), F32)
            value_sum[g, pl.ds(at, TILE), :] = jnp.zeros((TILE, HEAD), F32)
        for slot in range(2):

            @pl.when(lowest <= tops[slot])
            def _(slot=slot):
                mask = key_pos <= query_rows[slot]
                for g in range(KV_HEADS):
                    grads_tile(
                        rate_ref,
                        work_refs[slot],
                        final_ref,
                        key_c,
                        value_c,
                        key_sum,
                        value_sum,
                        query_sum,
                        mask,
                        at,
                        slot,
                        g,
                    )

        return 0

    lax.fori_loop(0, (length + TILE - 1) // TILE, tile, 0)
    row = lax.broadcasted_iota(jnp.int32, (ROWS, HEAD), 0)
    for slot, starts, counts in entries:
        for out, at, n in zip(outs, starts, counts):
            at = pl.multiple_of(at, 16)
            for g in range(KV_HEADS):
                lanes = slice(g * HEAD, (g + 1) * HEAD)
                for number, total in enumerate((key_sum, value_sum)):
                    out[slot, number * ROWS : (number + 1) * ROWS, lanes] = jnp.where(
                        row < n, total[g, pl.ds(at, ROWS), :], 0.0
                    )


def grads_body(count, is_first, is_last, *refs):
    rate_ref, own_ref, kept_ref, got_ref, final_ref = refs[:5]
    blocks = refs[5 : 5 + count]
    refs = refs[5 + count :]
    if not is_first:
        prior_ref, refs = refs[0], refs[1:]
    outs, refs = refs[:count], refs[count:]
    if is_last:
        query_outs, refs = refs[:2], refs[2:]
    query_sum, key_c, value_c, pos_c, key_sum, value_sum = refs
    query_rows, tops, first = query_side(own_ref)
    length, entries = place(
        blocks, first, jnp.maximum(tops[0], tops[1]), key_c, value_c, pos_c
    )
    if is_first:
        query_sum[...] = jnp.zeros_like(query_sum)
    elif is_last:
        query_sum[...] = prior_ref[...]

    grads_work(
        rate_ref,
        (kept_ref, got_ref),
        final_ref,
        key_c,
        value_c,
        pos_c,
        key_sum,
        value_sum,
        query_sum,
        query_rows,
        tops,
        length,
        entries,
        outs,
    )
    if is_last:
        for slot in range(2):
            for g in range(KV_HEADS):
                for head in range(GROUP):
                    lanes = slice(head * ROWS, (head + 1) * ROWS)
                    rows = slice((g * GROUP + head) * ROWS, (g * GROUP + head + 1) * ROWS)
                    query_outs[slot][rows, :] = query_sum[slot * KV_HEADS + g, :, lanes].T.astype(
                        BF16
                    )


def compact_scratch(count):
    size = 2 * count * ROWS + 2 * TILE
    return [
        pltpu.VMEM((KV_HEADS, size, HEAD), BF16),
        pltpu.VMEM((KV_HEADS, size, HEAD), BF16),
        pltpu.VMEM((size, ROWS), F32),
    ]


STATE = jax.ShapeDtypeStruct((2 * KV_HEADS, 5, 8, WIDE), F32)
PART = jax.ShapeDtypeStruct((2, 2 * ROWS, KV_HEADS * HEAD), F32)
SUMS = jax.ShapeDtypeStruct((2 * KV_HEADS, HEAD, WIDE), F32)
SMALL = jax.ShapeDtypeStruct((8, ROWS), F32)
FINAL = jax.ShapeDtypeStruct((2 * KV_HEADS, 8, WIDE), F32)


def stats(rate, own, kept, got, jobs, prior=None, is_last=False):
    if is_last:
        outs = [FINAL, SMALL, PART, SUMS]
        scratch = [pltpu.VMEM(STATE.shape, F32)]
    else:
        outs, scratch = [STATE, SMALL], []
    blocks = [block for some, _ in jobs for block in some]
    operands = [rate, own, kept, got, *blocks] + ([] if prior is None else [prior])
    sizes = [(len(some), slots) for some, slots in jobs]
    rest = []
    if is_last:
        size = 2 * ROWS + TILE
        rest = [pltpu.VMEM((KV_HEADS, size, HEAD), F32), pltpu.VMEM((KV_HEADS, size, HEAD), F32)]
    return call(
        functools.partial(stats_body, sizes, prior is None, is_last),
        outs,
        scratch + compact_scratch(max(count for count, _ in sizes)) + rest,
        sum(count * len(slots) for count, slots in sizes) * ROWS * 2 * HEADS * ROWS * HEAD * 4,
        4 << 20,
        [pl.BlockSpec(memory_space=pltpu.VMEM)] * len(operands),
    )(*operands)


def grads(rate, own, kept, got, final, blocks, prior=None, is_last=False):
    count = len(blocks)
    outs = [jax.ShapeDtypeStruct((2, 2 * ROWS, KV_HEADS * HEAD), F32)] * count
    sums = jax.ShapeDtypeStruct((2 * KV_HEADS, HEAD, WIDE), F32)
    operands = [rate, own, kept, got, final, *blocks]
    operands = operands + ([] if prior is None else [prior])
    if is_last:
        outs = outs + [jax.ShapeDtypeStruct((HEADS * ROWS, HEAD), BF16)] * 2
        scratch = [pltpu.VMEM(sums.shape, F32)]
    else:
        outs, scratch = outs + [sums], []
    aliases = {} if prior is None or is_last else {len(operands) - 1: len(outs) - 1}
    size = 2 * count * ROWS + TILE
    scratch = (
        scratch
        + compact_scratch(count)
        + [pltpu.VMEM((KV_HEADS, size, HEAD), F32), pltpu.VMEM((KV_HEADS, size, HEAD), F32)]
    )
    return call(
        functools.partial(grads_body, count, prior is None, is_last),
        outs,
        scratch,
        count * 2 * ROWS * 2 * HEADS * ROWS * 2 * HEAD * 5,
        6 << 20,
        [pl.BlockSpec(memory_space=pltpu.VMEM)] * len(operands),
        aliases=aliases,
    )(*operands)


def local(queries, keys, values, out_grad, routes, per_head_scale):
    me = lax.axis_index("ctx")
    size = lax.axis_size("ctx")
    ring = size // 2
    x = (me // ring).astype(jnp.int32)
    x_ref = x.reshape(1)
    across = [(i, (i + ring) % size) for i in range(size)]

    def neighbour(i, up):
        base, z = i // ring * ring, i % ring
        return base + (z + (1 if up == (z % 2 == 0) else -1)) % ring

    even = [(i, neighbour(i, True)) for i in range(size)]
    odd = [(i, neighbour(i, False)) for i in range(size)]

    def swap(array, pairs, axis="ctx"):
        return lax.ppermute(array, axis, pairs)

    smem = pl.BlockSpec(memory_space=pltpu.SMEM)
    vmem = pl.BlockSpec(memory_space=pltpu.VMEM)
    anywhere = pl.BlockSpec(memory_space=pl.ANY)
    in_hbm = pl.BlockSpec(memory_space=pltpu.HBM)
    width = KV_HEADS * HEAD
    message = jax.ShapeDtypeStruct((MESSAGE, width), BF16)
    keys_kept, keys_sent = call(
        pack_keys_body,
        [message, message],
        [
            pltpu.VMEM((ROWS, 2 * width), BF16),
            pltpu.VMEM((ROWS, 2 * width), BF16),
            pltpu.VMEM((1, ROWS), jnp.int32),
            pltpu.SemaphoreType.DMA((3,)),
        ],
        1024,
        1 << 20,
        [smem, in_hbm, in_hbm, in_hbm],
        60,
    )(x_ref, keys[0], values[0], routes)
    keys_got = swap(keys_sent, across)
    work = jax.ShapeDtypeStruct((2, HEADS * ROWS, HEAD), BF16)
    kept, sent = call(
        pack_queries_body,
        [work, work],
        [
            pltpu.VMEM((ROWS, 2 * HEADS * HEAD), BF16),
            pltpu.VMEM((ROWS, 2 * HEADS * HEAD), BF16),
            pltpu.SemaphoreType.DMA((2,)),
        ],
        1024,
        4 << 20,
        [smem, anywhere, in_hbm, in_hbm],
        60,
    )(x_ref, keys_sent, queries[0], out_grad[0])
    got = swap(sent, across)
    own = call(
        join_body,
        jax.ShapeDtypeStruct((2, MESSAGE, width), BF16),
        [],
        1024,
        1 << 20,
        [anywhere, vmem, vmem],
    )(sent, keys_kept, keys_got)

    half_scale = lax.dynamic_slice_in_dim(per_head_scale, x * HEADS, HEADS)
    rate = jnp.repeat(half_scale * (LOG2E / math.sqrt(HEAD)), ROWS).reshape(KV_HEADS, 1, WIDE)
    rate = jnp.broadcast_to(rate, (KV_HEADS, 8, WIDE))

    def gate(blocks, after):
        def body(*refs):
            for source, target in zip(refs, refs[len(blocks) + 1 :]):
                target[...] = source[...]

        return call(
            body,
            [jax.ShapeDtypeStruct(block.shape, block.dtype) for block in blocks],
            [],
            1024,
            1 << 20,
            [vmem] * (len(blocks) + 1),
        )(*blocks, after)

    a, b = [own], [own]
    a.append(swap(own, even))
    b.append(swap(own, odd))
    state, token = stats(rate, own, kept, kept, [([own], (0,))])
    a[1], b[1] = gate([a[1], b[1]], token)
    a.append(swap(b[1], even))
    b.append(swap(a[1], odd))
    state, token = stats(rate, own, kept, kept, [([a[1], b[1]], (0,))], state)
    a[2], b[2] = gate([a[2], b[2]], token)
    a.append(swap(b[2], even))
    b.append(swap(a[2], odd))
    state, token = stats(rate, own, kept, kept, [([a[2], b[2]], (0,))], state)
    a[3], b[3] = gate([a[3], b[3]], token)
    a.append(swap(b[3], even))
    jobs = [([own, a[1], b[1], a[2], b[2]], (1,)), ([a[3], b[3]], (0, 1))]
    state, token = stats(rate, own, kept, got, jobs, state)
    final, scale, far, sums = stats(rate, own, kept, got, [([a[4]], (0, 1))], state, is_last=True)

    total_devices = lax.axis_size("dp") * size

    def exchange(array, masks):
        pairs = [[(i, i ^ mask) for i in range(total_devices)] for mask in masks]
        return [array] + [swap(array, pair, ("dp", "ctx")) for pair in pairs]

    def hop(step, parts, arrived, scales=()):
        out = jax.ShapeDtypeStruct((2, 2 * ROWS + (32 if step > 1 else 0), width), BF16)
        return call(
            functools.partial(hop_body, step, len(scales)),
            [out, out, SMALL],
            [],
            1024,
            2 << 20,
            [vmem] * (2 + len(arrived) + len(scales)),
        )(*parts, *arrived, *scales)

    scales = exchange(scale, (4,))
    from_even = swap(far.astype(BF16), even)
    part_a, part_b, sums = grads(rate, own, kept, got, final, [a[3], b[3]], sums)
    to_a, to_b, scale = hop(3, (part_a, part_b), (from_even,), scales)
    sent_a, sent_b = swap(to_a, even), swap(to_b, odd)
    part_a, part_b, near, sums = grads(rate, own, kept, got, final, [a[2], b[2], own], sums)
    to_a, to_b, beside = hop(2, (part_a, part_b), (sent_a, sent_b))
    sent_a, sent_b = swap(to_a, even), swap(to_b, odd)
    part_a, part_b, query_kept, query_sent = grads(
        rate, own, kept, got, final, [a[1], b[1]], sums, is_last=True
    )
    query_got = swap(query_sent, across)
    to_a, to_b, scale = hop(1, (part_a, part_b), (sent_a, sent_b), [scale, beside])
    sent_a, sent_b = swap(to_a, even), swap(to_b, odd)
    scales = exchange(scale, (8,))
    scales = exchange(scales[0] + scales[1], (16, 32, 48))
    ours, theirs, scale = call(
        last_hop_body,
        [jax.ShapeDtypeStruct((2 * ROWS, width), BF16)] * 2 + [SMALL],
        [],
        1024,
        2 << 20,
        [vmem] * 7,
    )(near, sent_a, sent_b, *scales)
    other = swap(theirs, across)
    scales = exchange(scale, (64, 128, 192))
    query_out, key_out, value_out, scale_out = call(
        finish_body,
        [
            jax.ShapeDtypeStruct((ROWS, 2 * HEADS * HEAD), BF16),
            jax.ShapeDtypeStruct((ROWS, 2 * width), BF16),
            jax.ShapeDtypeStruct((ROWS, 2 * width), BF16),
            jax.ShapeDtypeStruct((1, 2 * HEADS), F32),
        ],
        [],
        1024,
        2 << 20,
        [smem] + [vmem] * 8,
    )(x_ref, query_kept, query_got, ours, other, *scales)
    return query_out[None], key_out[None], value_out[None], scale_out.reshape(2 * HEADS)


def solution(mesh):
    in_specs = (
        P("dp", "ctx", None),
        P("dp", "ctx", None),
        P("dp", "ctx", None),
        P("dp", "ctx", None),
        P("dp", "ctx"),
        P(),
    )
    out_specs = (P("dp", "ctx", None), P("dp", "ctx", None), P("dp", "ctx", None), P())
    return jax.shard_map(local, mesh=mesh, in_specs=in_specs, out_specs=out_specs, check_vma=False)
```
